256 devices in a mesh: section: 8 (over x, y_lo), expert: 16 (over y_hi, z), dp: 2 (over core).
Axes of the slice: x: 4, y: 4 (y_hi: 2, y_lo: 2; y = y_hi * 2 + y_lo), z: 8, core: 2. Of those that a mesh axis runs over, the one named last changes fastest.
Arguments:
- saved_rows: bfloat16 [8, 4096, 4096], P('section', ('expert', 'dp')), may hold values from -6 to 6
- grad_out: bfloat16 [8, 4096, 4096], P('section', ('expert', 'dp')), may hold values from -6 to 6
- expert_ids: int32 [8, 4096, 1], P('section', ('expert', 'dp')), may hold values from 0 to 3; in each aligned block of 128 rows (0 to 127, 128 to 255, ..., all dimensions but the last counted through in order) at most 48 rows name the same one
- combine: float32 [8, 4096, 1], P('section', ('expert', 'dp')), may hold values from 0.25 to 1
- w_gate: bfloat16 [8, 4096, 6144], P('section', 'dp', 'expert'), may hold values from -0.09375 to 0.09375
- w_up: bfloat16 [8, 4096, 6144], P('section', 'dp', 'expert'), may hold values from -0.09375 to 0.09375
- w_down: bfloat16 [8, 6144, 4096], P('section', 'expert', 'dp'), may hold values from -0.15625 to 0.15625
Outputs:
- grad_in: bfloat16 [8, 4096, 4096], P('section', ('expert', 'dp'))
- grad_gate: bfloat16 [8, 4096, 6144], P('section', 'dp', 'expert')
- grad_up: bfloat16 [8, 4096, 6144], P('section', 'dp', 'expert')
- grad_down: bfloat16 [8, 6144, 4096], P('section', 'expert', 'dp')
The draws below stay inside these ranges and needn't reach their ends.
Inputs may be any that keep to these rules, and one draw needn't show every extreme that they name: `expert_ids`: within the 128 rows of one device no expert is chosen more than 48 times, and in every draw some device's rows choose one expert exactly 48 times.
All inputs are finite; a program needn't handle non-finite values.
Results may differ from the reference program's by a relative error of at most 0.0065.
Values may be sent and summed in bfloat16 or wider, within the bound.
A program may use at most 128 MiB of HBM per device.

```python
import math
import jax
import jax.numpy as jnp
import numpy as np
from jax import lax

D = 4096
FF = 1536
TOK_DEV = 128
EXPERTS = 4
TOPK = 1
CAP = 48
TOK_SECTION = 4096
N_SECTION = 8
N_EXPERT = 16
N_DP = 2


def level_of(stream_key, dims, pieces, low, high):
    def one(axis_at, blocks):
        steps = jax.random.uniform(jax.random.fold_in(jax.random.fold_in(stream_key, 6), axis_at), (blocks,), jnp.float32, low / len(pieces), high / len(pieces))
        return jnp.repeat(jnp.exp(steps), dims[axis_at] // blocks).reshape((-1,) + (1,) * (len(dims) - axis_at - 1))

    factor_of = one(*pieces[0])
    for cut in pieces[1:]:
        factor_of = factor_of * one(*cut)
    return factor_of


def routed_block(stream_key, own, number, rows, number_of, top, limit, slope):
    order = jax.random.permutation(stream_key, number_of)
    heavy_load, usual = load_shares(number_of, rows * top, limit, slope, True), load_shares(number_of, rows * top, limit, slope, False)
    places = jnp.arange(number_of)

    def named(tallies, rotation):
        used = int((tallies > 0).sum())
        fixed = max(1, used // 4)
        moved = fixed + (places - fixed + rotation * (used - fixed)) % max(1, number_of - fixed)
        return jnp.zeros((number_of,), jnp.int32).at[order[jnp.where(places < fixed, places, moved)]].set(jnp.asarray(tallies, jnp.int32))

    tallies = jnp.where(number % 4 == 0, named(heavy_load, number // 4), named(usual, number - number // 4 - 1))
    mixed = jax.random.permutation(jax.random.fold_in(own, 3), number_of)
    giver, taker = mixed[0:number_of // 2 * 2:2], mixed[1:number_of // 2 * 2:2]
    margin = jnp.minimum(tallies[giver] - 1, limit - tallies[taker]) // 2
    margin = jnp.where((giver == order[0]) | (taker == order[0]) | (tallies[taker] == 0), 0, jnp.maximum(margin, 0))
    moved = jax.random.randint(jax.random.fold_in(own, 4), (number_of // 2,), 0, 1 << 20) % (margin + 1)
    tallies = tallies.at[giver].add(-moved).at[taker].add(moved)
    members = jnp.searchsorted(jnp.cumsum(tallies), jnp.arange(rows * top), side="right").astype(jnp.int32)
    table = members.reshape(top, rows).T
    table = table[jax.random.permutation(jax.random.fold_in(own, 1), rows)]
    rotation = jax.random.randint(jax.random.fold_in(own, 2), (rows, 1), 0, top)
    return jnp.take_along_axis(table, (jnp.arange(top)[None, :] + rotation) % top, axis=1)


def load_shares(amount, total, bound, slope, full):
    weights = [(1 << 20) // math.isqrt(grade ** slope) + 1 for grade in range(1, amount + 1)]
    largest = bound if full else min(bound, max(-(-total // amount), total * weights[0] // sum(weights)))
    least = 1 if total - largest >= amount - 1 else 0
    holding, surplus = [largest] + [least] * (amount - 1), total - largest - least * (amount - 1)
    while surplus > 0:
        free = [i for i in range(1, amount) if holding[i] < largest] or [i for i in range(1, amount) if holding[i] < bound]
        mass, remaining = sum([weights[i] for i in free]), surplus
        for i in free:
            addition = min(bound - holding[i], max(1, remaining * weights[i] // mass), surplus)
            holding[i] = holding[i] + addition
            surplus = surplus - addition
    return np.array(holding)


def noise(rng, shape, width, limit, cuts=(), kind=jnp.bfloat16):
    drawn = width * jax.random.normal(rng, shape, jnp.float32)
    if cuts:
        drawn = drawn * level_of(rng, shape, cuts, -0.22, 0.18)
    return jnp.clip(drawn, -limit, limit).astype(kind)


def setup_inputs(seed: int = 0) -> dict:
    key_of = jax.random.split(jax.random.key(seed), 8)
    saved_rows = noise(key_of[0], (N_SECTION, TOK_SECTION, D), 1.0, 6.0, ((0, 8), (1, 32)))
    grad_out = noise(key_of[1], (N_SECTION, TOK_SECTION, D), 1.0, 6.0, ((0, 8), (1, 32)))
    expert_ids_keys = jax.random.split(jax.random.fold_in(key_of[2], 1), N_SECTION * TOK_SECTION // TOK_DEV)
    expert_ids_turns = jax.random.permutation(jax.random.fold_in(key_of[2], 3), N_SECTION * TOK_SECTION // TOK_DEV)
    expert_ids = jax.vmap(lambda own, number: routed_block(jax.random.fold_in(key_of[2], 2), own, number, TOK_DEV, EXPERTS, TOPK, CAP, 2))(expert_ids_keys, expert_ids_turns).reshape((N_SECTION, TOK_SECTION, TOPK))
    combine = jnp.clip(0.25 + 0.75 * jax.random.uniform(key_of[3], (N_SECTION, TOK_SECTION, TOPK), jnp.float32) ** level_of(key_of[3], (N_SECTION, TOK_SECTION, TOPK), ((0, 8), (1, 32)), -0.2, 0.2), 0.25, 1.0)
    w_gate = noise(key_of[4], (N_SECTION, D, EXPERTS * FF), D ** -0.5, 0.09375, ((0, 8), (1, 2), (2, 16)))
    w_up = noise(key_of[5], (N_SECTION, D, EXPERTS * FF), D ** -0.5, 0.09375, ((0, 8), (1, 2), (2, 16)))
    w_down = noise(key_of[6], (N_SECTION, EXPERTS * FF, D), FF ** -0.5, 0.15625, ((0, 8), (1, 16), (2, 2)))
    return dict(saved_rows=saved_rows, grad_out=grad_out, expert_ids=expert_ids, combine=combine, w_gate=w_gate, w_up=w_up, w_down=w_down)


def round_trip(values):
    return lax.optimization_barrier(values.astype(jnp.bfloat16)).astype(jnp.float32)


def reference(saved_rows, grad_out, expert_ids, combine, w_gate, w_up, w_down):
    shares = N_EXPERT // EXPERTS
    share_units = FF // shares
    slot_total = N_EXPERT * CAP
    inputs_all = []
    gates_all = []
    ups_all = []
    downs_all = []
    for section_no in range(N_SECTION):
        tok_rows = saved_rows[N_SECTION - 1 - section_no].reshape(N_EXPERT, N_DP, TOK_DEV, D)
        tok_grads = grad_out[section_no].reshape(N_EXPERT, N_DP, TOK_DEV, D)
        chosen_all = expert_ids[section_no, :, 0].reshape(N_EXPERT, N_DP, TOK_DEV)
        weights_all = combine[section_no, :, 0].reshape(N_EXPERT, N_DP, TOK_DEV)
        sum_gate = jnp.zeros((D, EXPERTS * FF), jnp.float32)
        sum_up = jnp.zeros((D, EXPERTS * FF), jnp.float32)
        sum_down = jnp.zeros((EXPERTS * FF, D), jnp.float32)
        replica_grads = []
        for replica in range(N_DP):
            chosen = chosen_all[:, replica]
            choose = (chosen[:, :, None] == jnp.arange(EXPERTS, dtype=jnp.int32)).astype(jnp.int32)
            before = jnp.cumsum(choose, axis=1) - choose
            slot_of = jnp.sum(before * choose, axis=2).astype(jnp.int32)
            source_of = jnp.broadcast_to(jnp.arange(N_EXPERT, dtype=jnp.int32)[:, None], chosen.shape)
            scaled = (weights_all[:, replica][:, :, None] * tok_grads[:, replica].astype(jnp.float32)).astype(jnp.bfloat16)
            packed_in = jnp.zeros((EXPERTS, N_EXPERT, CAP, D), jnp.bfloat16).at[chosen, source_of, slot_of].set(tok_rows[:, replica])
            packed_grad = jnp.zeros((EXPERTS, N_EXPERT, CAP, D), jnp.bfloat16).at[chosen, source_of, slot_of].set(scaled)
            expert_grads = []
            gate_parts = []
            up_parts = []
            down_parts = []
            for expert in range(EXPERTS):
                rows_in = packed_in[expert].reshape(slot_total, D)
                rows_grad = packed_grad[expert].reshape(slot_total, D)
                gate_mat = w_gate[section_no][:, expert * FF:(expert + 1) * FF]
                up_mat = w_up[section_no][:, expert * FF:(expert + 1) * FF]
                down_mat = w_down[section_no][expert * FF:(expert + 1) * FF, :]
                gate_proj = jnp.dot(rows_in, gate_mat, preferred_element_type=jnp.float32)
                up_proj = jnp.dot(rows_in, up_mat, preferred_element_type=jnp.float32)
                back_grad = jnp.dot(rows_grad, down_mat.T, preferred_element_type=jnp.float32)
                sigmoid = jax.nn.sigmoid(gate_proj)
                active = gate_proj * sigmoid
                hidden = (active * up_proj).astype(jnp.bfloat16)
                d_gate = (back_grad * up_proj * sigmoid * (1.0 + gate_proj * (1.0 - sigmoid))).astype(jnp.bfloat16)
                d_upper = (back_grad * active).astype(jnp.bfloat16)
                share_list = []
                for share in range(shares):
                    lower = share * share_units
                    upper_end = lower + share_units
                    part_gate = jnp.dot(d_gate[:, lower:upper_end], gate_mat[:, lower:upper_end].T, preferred_element_type=jnp.float32)
                    part_up = jnp.dot(d_upper[:, lower:upper_end], up_mat[:, lower:upper_end].T, preferred_element_type=jnp.float32)
                    share_list.append(round_trip(part_gate + part_up))
                summed = share_list[0]
                for extra in share_list[1:]:
                    summed = summed + extra
                expert_grads.append(summed.astype(jnp.bfloat16).reshape(N_EXPERT, CAP, D))
                gate_parts.append(jnp.dot(rows_in.T, d_gate, preferred_element_type=jnp.float32))
                up_parts.append(jnp.dot(rows_in.T, d_upper, preferred_element_type=jnp.float32))
                down_parts.append(jnp.dot(hidden.T, rows_grad, preferred_element_type=jnp.float32))
            sum_gate = sum_gate + round_trip(jnp.concatenate(gate_parts, axis=1))
            sum_up = sum_up + round_trip(jnp.concatenate(up_parts, axis=1))
            sum_down = sum_down + round_trip(jnp.concatenate(down_parts, axis=0))
            stacked = jnp.stack(expert_grads)
            replica_grads.append(stacked[chosen, source_of, slot_of])
        inputs_all.append(jnp.stack(replica_grads, axis=1).reshape(N_EXPERT * N_DP * TOK_DEV, D))
        gates_all.append(sum_gate.astype(jnp.bfloat16))
        ups_all.append(sum_up.astype(jnp.bfloat16))
        downs_all.append(sum_down.astype(jnp.bfloat16))
    return (jnp.stack(inputs_all), jnp.stack(gates_all), jnp.stack(ups_all), jnp.stack(downs_all))
```

```python
import functools

import jax
import jax.numpy as jnp
from jax import lax
from jax.experimental import pallas as pl
from jax.experimental.pallas import tpu as pltpu
from jax.sharding import PartitionSpec as P

EXPERTS = 4
CAP = 48
SHARES = 4
RING = 8
STEPS = 9
COLS = 256
MESH = pl.DeviceIdType.MESH
F32 = jnp.float32
BF16 = jnp.bfloat16


def dot(a, b, dim_a, dim_b):
    return lax.dot_general(a, b, (((dim_a,), (dim_b,)), ((), ())), preferred_element_type=F32)


def kernel(
    px, pz, wg, wu, wd,
    f_out, gg_out, gu_out, gd_out,
    xb, zb, wgu, wdn, pb, rb, d2, hd, g1, g2,
    rx, ent_send, fwd_send, rr, rsend, fr, wrecv, wsend, wloc, grecv, gsend, gloc,
):
    sec, k, rep = lax.axis_index("section"), lax.axis_index("expert"), lax.axis_index("dp")
    mirror = lax.axis_size("section") - 1 - sec
    yh, z = k // RING, k % RING
    seg, c = z // SHARES, z % SHARES
    mine = 2 * yh + seg
    other = 1 - rep
    width = xb.shape[-1]
    half = width // 2
    units = hd.shape[-1]

    def zof(pos):
        return (SHARES * seg + pos + RING) % RING

    def here(expert):
        return (sec, expert, rep)

    twin = (sec, k, other)

    def remote(src, dst, send, recv, dev):
        return pltpu.make_async_remote_copy(
            src_ref=src, dst_ref=dst, send_sem=send, recv_sem=recv, device_id=dev, device_id_type=MESH
        )

    def entry(e, t):
        ye, te = e // 2, e % 2
        far = jnp.where(c < 2, SHARES - 1, 0)
        z_in = jnp.where(seg == te, z, te * SHARES + far)
        src, buf, s = ((px, xb, mirror), (pz, zb, sec))[t]
        return remote(
            src.at[e], buf.at[z, yh], ent_send.at[t, e], rx.at[t, z], (s, ye * RING + z_in, rep)
        )

    own_copy = [
        pltpu.make_async_copy(pz.at[e], zb.at[z, yh], rx.at[1, z]) for e in range(EXPERTS)
    ]
    for e in range(EXPERTS):
        @pl.when(mine == e)
        def _():
            own_copy[e].start()

        @pl.when(mine != e)
        def _():
            entry(e, 1).start()
    for e in range(EXPERTS):
        entry(e, 0).start()

    rows = pl.ds(pl.multiple_of(rep * half, half), half)
    rows_far = pl.ds(pl.multiple_of(other * half, half), half)
    w_parts = (
        (wg, lambda r: wgu.at[r, pl.ds(0, units)]),
        (wu, lambda r: wgu.at[r, pl.ds(units, units)]),
        (wd, lambda r: wdn.at[:, r]),
    )
    for i, (src, dst) in enumerate(w_parts):
        pltpu.make_async_copy(src, dst(rows), wloc.at[i]).start()
        remote(src, dst(rows), wsend.at[i], wrecv.at[i], twin).start()

    right, left = here(k + 1), here(k - 1)

    def forward(t, buf, side, zz):
        return remote(
            buf.at[zz], buf.at[zz], fwd_send.at[t, side, zz], rx.at[t, zz], (left, right)[side]
        )

    def arrive(pos, go_left, go_right):
        zz = zof(pos)
        for t, buf in ((1, zb), (0, xb)):
            remote(
                buf.at[zz], buf.at[zz], fwd_send.at[t, 0, zz], rx.at[t, zz], twin
            ).wait_recv()
            for side, go in ((1, go_right), (0, go_left)):
                if go is not None:
                    @pl.when(go)
                    def _():
                        forward(t, buf, side, zz).start()

    def compute(zz):
        n_rows = 2 * CAP
        x = xb[zz].reshape(n_rows, width)
        gu = dot(x, wgu[...], 1, 0)
        back = dot(zb[zz].reshape(n_rows, width), wdn[...], 1, 1)
        gate, up = gu[:, :units], gu[:, units:]
        sig = jax.nn.sigmoid(gate)
        act = gate * sig
        hd[zz] = (act * up).astype(BF16)
        d_gate = (back * up * sig * (1.0 + gate * (1.0 - sig))).astype(BF16)
        d_up = (back * act).astype(BF16)
        d2[zz, :, :units] = d_gate
        d2[zz, :, units:] = d_up
        d = jnp.concatenate([d_gate, d_up], axis=1)
        chunk = 1024

        def part(n, _):
            cols = pl.ds(pl.multiple_of(n * chunk, chunk), chunk)
            pb[zz, :, :, cols] = dot(d, wgu[cols, :], 1, 1).astype(BF16).reshape(2, CAP, chunk)

        lax.fori_loop(0, width // chunk, part, None)

    def go_back(src, zz, side, at_end):
        slot = jnp.where(at_end, RING, zz) if side else zz
        return remote(
            src.at[zz], rb.at[slot], rsend.at[0, zz], rr.at[slot], (left, right)[side]
        )

    def go_home(src, zz, y):
        return remote(
            src.at[zz, y], f_out.at[mine], rsend.at[y, zz], fr.at[mine], here(y * RING + zz)
        )

    def add_part(zz):
        for y in range(2):
            rb[zz, y] = (rb[zz, y].astype(F32) + pb[zz, y].astype(F32)).astype(BF16)

    def wait_back(slot):
        remote(rb.at[slot], rb.at[slot], rsend.at[0, 0], rr.at[slot], twin).wait_recv()

    def step_conditions(j):
        in_left = (j >= 1) & (j <= c + 2)
        in_right = (j >= 1) & (j <= 5 - c)
        p_from_right = 6 - c - j
        p_from_left = j - c
        from_right = (c < 3) & (p_from_right >= -2) & (p_from_right <= c)
        from_left = (c > 0) & (p_from_left >= c) & (p_from_left <= 5)
        finish = j == jnp.where((c == 0) | (c == 3), 6, 4)
        return in_left, in_right, p_from_right, p_from_left, from_right, from_left, finish

    def home_copy():
        return pltpu.make_async_copy(pb.at[z, yh], f_out.at[mine], fr.at[mine])

    def weight_cols(m):
        return pl.ds(pl.multiple_of(m * COLS, COLS), COLS)

    n_all = RING * 2 * CAP

    def grads_in(m, _):
        cols = weight_cols(m)
        xt = xb[:, :, :, cols].reshape(n_all, COLS)
        wgu[cols, :] = dot(xt, d2[...].reshape(n_all, 2 * units), 0, 0).astype(BF16)

    def grads_down(m, _):
        cols = weight_cols(m)
        zt = zb[:, :, :, cols].reshape(n_all, COLS)
        wdn[:, cols] = dot(hd[...].reshape(n_all, units), zt, 0, 0).astype(BF16)

    per_half = half // COLS
    send_in = remote(wgu.at[rows_far], g1, gsend.at[0], grecv.at[0], twin)
    send_down = remote(wdn.at[:, rows_far], g2, gsend.at[1], grecv.at[1], twin)

    def step(j, _):
        in_left, in_right, p_r, p_l, from_right, from_left, finish = step_conditions(j)

        @pl.when(j == 0)
        def _():
            arrive(c, c > 0, c < 3)

        @pl.when(in_left)
        def _():
            arrive(c - j, None, c < 3)

        @pl.when(in_right)
        def _():
            arrive(c + j, c > 0, None)

        @pl.when(j == 0)
        def _():
            for i, (src, dst) in enumerate(w_parts):
                pltpu.make_async_copy(src, dst(rows), wloc.at[i]).wait()
                remote(src, dst(rows_far), wsend.at[i], wrecv.at[i], twin).wait_recv()

        def side_step(side, _):
            pos = jnp.where(side == 0, c - j, c + j)
            valid = jnp.where(side == 0, (j == 0) | in_left, in_right)

            @pl.when(valid)
            def _():
                zz = zof(pos)
                compute(zz)

                @pl.when((j > 0) & (side == 0) & (c == 3))
                def _():
                    go_back(pb, zz, 0, False).start()

                @pl.when((side == 1) & (c == 0))
                def _():
                    go_back(pb, zz, 1, pos == 1).start()

        lax.fori_loop(0, 2, side_step, None)

        @pl.when(from_right)
        def _():
            zz = zof(p_r)
            wait_back(zz)

            @pl.when(p_r < c)
            def _():
                add_part(zz)

                @pl.when(c > 0)
                def _():
                    go_back(rb, zz, 0, False).start()

                @pl.when(c == 0)
                def _():
                    for y in range(2):
                        go_home(rb, zz, y).start()

        @pl.when(from_left)
        def _():
            zz = zof(p_l)

            @pl.when(p_l == c)
            def _():
                wait_back(RING)

            @pl.when(p_l > c)
            def _():
                wait_back(zz)
                add_part(zz)

                @pl.when(c < 3)
                def _():
                    go_back(rb, zz, 1, p_l == c + 1).start()

                @pl.when(c == 3)
                def _():
                    for y in range(2):
                        go_home(rb, zz, y).start()

        @pl.when(finish)
        def _():
            for y in range(2):
                @pl.when(c == 0)
                def _():
                    pb[z, y] = (pb[z, y].astype(F32) + rb[z, y].astype(F32)).astype(BF16)

                @pl.when(c == 3)
                def _():
                    pb[z, y] = (pb[z, y].astype(F32) + rb[RING, y].astype(F32)).astype(BF16)

                @pl.when((c > 0) & (c < 3))
                def _():
                    total = pb[z, y].astype(F32) + rb[z, y].astype(F32)
                    pb[z, y] = (total + rb[RING, y].astype(F32)).astype(BF16)

            home_copy().start()
            go_home(pb, z, 1 - yh).start()

        @pl.when(j == 5)
        def _():
            lax.fori_loop(other * per_half, (other + 1) * per_half, grads_in, None)
            send_in.start()

        @pl.when(j == 6)
        def _():
            lax.fori_loop(other * per_half, (other + 1) * per_half, grads_down, None)
            send_down.start()
            lax.fori_loop(rep * per_half, (rep + 1) * per_half, grads_in, None)

        @pl.when(j == 7)
        def _():
            lax.fori_loop(rep * per_half, (rep + 1) * per_half, grads_down, None)

    lax.fori_loop(0, STEPS, step, None)

    piece = 512

    send_in.wait_recv()

    def add_in(m, _):
        at = pl.ds(pl.multiple_of(m * piece, piece), piece)
        own = wgu[pl.ds(pl.multiple_of(rep * half + m * piece, piece), piece), :]
        g1[at, :] = (g1[at, :].astype(F32) + own.astype(F32)).astype(BF16)

    lax.fori_loop(0, half // piece, add_in, None)
    outs = [
        pltpu.make_async_copy(g1.at[:, pl.ds(0, units)], gg_out, gloc.at[0]),
        pltpu.make_async_copy(g1.at[:, pl.ds(units, units)], gu_out, gloc.at[1]),
        pltpu.make_async_copy(g2, gd_out, gloc.at[2]),
    ]
    outs[0].start()
    outs[1].start()
    send_down.wait_recv()

    def add_down(m, _):
        at = pl.ds(pl.multiple_of(m * piece, piece), piece)
        own = wdn[:, pl.ds(pl.multiple_of(rep * half + m * piece, piece), piece)]
        g2[:, at] = (g2[:, at].astype(F32) + own.astype(F32)).astype(BF16)

    lax.fori_loop(0, half // piece, add_down, None)
    outs[2].start()

    for e in range(EXPERTS):
        remote(f_out.at[e], f_out.at[e], rsend.at[0, 0], fr.at[e], twin).wait_recv()

    for e in range(EXPERTS):
        entry(e, 0).wait_send()

        @pl.when(mine != e)
        def _():
            entry(e, 1).wait_send()
    for i, (src, dst) in enumerate(w_parts):
        remote(src, dst(rows), wsend.at[i], wrecv.at[i], twin).wait_send()
    send_in.wait_send()
    send_down.wait_send()

    def drain(j, _):
        in_left, in_right, p_r, p_l, from_right, from_left, finish = step_conditions(j)

        def forwarded(go, side, pos):
            @pl.when(go)
            def _():
                for t, buf in ((1, zb), (0, xb)):
                    forward(t, buf, side, zof(pos)).wait_send()

        forwarded(((j == 0) | in_left) & (c < 3), 1, c - j)
        forwarded(((j == 0) | in_right) & (c > 0), 0, c + j)

        @pl.when(in_left & (c == 3))
        def _():
            go_back(pb, zof(c - j), 0, False).wait_send()

        @pl.when(in_right & (c == 0))
        def _():
            go_back(pb, zof(c + j), 1, False).wait_send()

        @pl.when(from_right & (p_r < c) & (c > 0))
        def _():
            go_back(rb, zof(p_r), 0, False).wait_send()

        @pl.when(from_right & (p_r < c) & (c == 0))
        def _():
            for y in range(2):
                go_home(rb, zof(p_r), y).wait_send()

        @pl.when(from_left & (p_l > c) & (c < 3))
        def _():
            go_back(rb, zof(p_l), 1, False).wait_send()

        @pl.when(from_left & (p_l > c) & (c == 3))
        def _():
            for y in range(2):
                go_home(rb, zof(p_l), y).wait_send()

        @pl.when(finish)
        def _():
            go_home(pb, z, 1 - yh).wait_send()

    lax.fori_loop(0, STEPS, drain, None)
    for out in outs:
        out.wait()


def placing_of(chosen):
    n_tok = chosen.shape[0]
    choose = chosen[:, None] == jnp.arange(EXPERTS, dtype=jnp.int32)[None, :]
    tok = jnp.arange(n_tok, dtype=jnp.int32)
    lower = (tok[:, None] > tok[None, :]).astype(BF16)
    before = dot(lower, choose.astype(BF16), 1, 0)
    slot = jnp.sum(jnp.where(choose, before, 0.0), axis=1).astype(jnp.int32)
    target = chosen * CAP + slot
    return (jnp.arange(EXPERTS * CAP, dtype=jnp.int32)[:, None] == target[None, :]).astype(BF16)


def body(saved_rows, grad_out, expert_ids, combine, w_gate, w_up, w_down):
    n_sec = lax.axis_size("section")
    chosen = expert_ids[0, :, 0]
    chosen_far = lax.ppermute(chosen, "section", [(i, n_sec - 1 - i) for i in range(n_sec)])
    width = saved_rows.shape[2]
    units = w_gate.shape[2]
    placing = placing_of(chosen)
    scaled = (combine[0] * grad_out[0].astype(F32)).astype(BF16)
    pz = dot(placing, scaled, 1, 0).astype(BF16).reshape(EXPERTS, CAP, width)
    px = dot(placing_of(chosen_far), saved_rows[0], 1, 0).astype(BF16)
    px = px.reshape(EXPERTS, CAP, width)
    half = width // 2
    dma = pltpu.SemaphoreType.DMA
    outs = pl.pallas_call(
        kernel,
        out_shape=(
            jax.ShapeDtypeStruct((EXPERTS, CAP, width), BF16),
            jax.ShapeDtypeStruct((half, units), BF16),
            jax.ShapeDtypeStruct((half, units), BF16),
            jax.ShapeDtypeStruct((units, half), BF16),
        ),
        in_specs=[pl.BlockSpec(memory_space=pl.ANY)] * 5,
        out_specs=[pl.BlockSpec(memory_space=pl.ANY)] * 4,
        scratch_shapes=[
            pltpu.VMEM((RING, 2, CAP, width), BF16),
            pltpu.VMEM((RING, 2, CAP, width), BF16),
            pltpu.VMEM((width, 2 * units), BF16),
            pltpu.VMEM((units, width), BF16),
            pltpu.VMEM((RING, 2, CAP, width), BF16),
            pltpu.VMEM((RING + 1, 2, CAP, width), BF16),
            pltpu.VMEM((RING, 2 * CAP, 2 * units), BF16),
            pltpu.VMEM((RING, 2 * CAP, units), BF16),
            pltpu.VMEM((half, 2 * units), BF16),
            pltpu.VMEM((units, half), BF16),
            dma((2, RING)),
            dma((2, EXPERTS)),
            dma((2, 2, RING)),
            dma((RING + 1,)),
            dma((2, RING)),
            dma((EXPERTS,)),
            dma((3,)),
            dma((3,)),
            dma((3,)),
            dma((2,)),
            dma((2,)),
            dma((3,)),
        ],
        compiler_params=pltpu.CompilerParams(
            has_side_effects=True, vmem_limit_bytes=60 * 1024 * 1024
        ),
    )(px, pz, w_gate[0], w_up[0], w_down[0])
    merged, grad_gate, grad_up, grad_down = outs
    grad_in = dot(placing, merged.reshape(EXPERTS * CAP, width), 0, 0).astype(BF16)
    return grad_in[None], grad_gate[None], grad_up[None], grad_down[None]


def solution(mesh):
    return jax.shard_map(
        body,
        mesh=mesh,
        in_specs=(
            P("section", ("expert", "dp"), None),
            P("section", ("expert", "dp"), None),
            P("section", ("expert", "dp"), None),
            P("section", ("expert", "dp"), None),
            P("section", "dp", "expert"),
            P("section", "dp", "expert"),
            P("section", "expert", "dp"),
        ),
        out_specs=(
            P("section", ("expert", "dp"), None),
            P("section", "dp", "expert"),
            P("section", "dp", "expert"),
            P("section", "expert", "dp"),
        ),
        check_vma=False,
    )
```

```python
import functools

import jax
import jax.numpy as jnp
from jax import lax
from jax.experimental import pallas as pl
from jax.experimental.pallas import tpu as pltpu
from jax.sharding import PartitionSpec as P

EXPERTS = 4
CAP = 48
SHARES = 4
RING = 8
STEPS = 12
LAG = 3
X_ENTERS = 0
COLS = 256
MESH = pl.DeviceIdType.MESH
F32 = jnp.float32
BF16 = jnp.bfloat16


def dot(a, b, dim_a, dim_b):
    return lax.dot_general(a, b, (((dim_a,), (dim_b,)), ((), ())), preferred_element_type=F32)


def kernel(
    px, pz, wg, wu, wd,
    f_out, gg_out, gu_out, gd_out,
    xb, zb, wgu, wdn, pb, rb, d2, hd, g1, g2,
    rx, ent_send, fwd_send, rr, rsend, fr, wrecv, wsend, wloc, grecv, gsend, gloc,
):
    sec, k, rep = lax.axis_index("section"), lax.axis_index("expert"), lax.axis_index("dp")
    mirror = lax.axis_size("section") - 1 - sec
    yh, z = k // RING, k % RING
    seg, c = z // SHARES, z % SHARES
    mine = 2 * yh + seg
    other = 1 - rep
    width = xb.shape[-1]
    half = width // 2
    units = hd.shape[-1]

    def zof(pos):
        return (SHARES * seg + pos + RING) % RING

    def here(expert):
        return (sec, expert, rep)

    twin = (sec, k, other)

    def remote(src, dst, send, recv, dev):
        return pltpu.make_async_remote_copy(
            src_ref=src, dst_ref=dst, send_sem=send, recv_sem=recv, device_id=dev, device_id_type=MESH
        )

    def entry(e, t):
        ye, te = e // 2, e % 2
        far = jnp.where(c < 2, SHARES - 1, 0)
        z_in = jnp.where(seg == te, z, te * SHARES + far)
        src, buf, s = ((px, xb, mirror), (pz, zb, sec))[t]
        return remote(
            src.at[e], buf.at[z, yh], ent_send.at[t, e], rx.at[t, z, yh], (s, ye * RING + z_in, rep)
        )

    def own_copy(e):
        return pltpu.make_async_copy(pz.at[e], zb.at[z, yh], rx.at[1, z, yh])

    def enter(t):
        for away in (False, True):
            for e in range(EXPERTS):
                go = (e % 2 != seg) if away else (e % 2 == seg)

                @pl.when(go if t == 0 else go & (mine != e))
                def _():
                    entry(e, t).start()

    for e in range(EXPERTS):
        @pl.when(mine == e)
        def _():
            own_copy(e).start()
    enter(1)

    rows = pl.ds(pl.multiple_of(rep * half, half), half)
    rows_far = pl.ds(pl.multiple_of(other * half, half), half)
    w_parts = (
        (wg, lambda r: wgu.at[r, pl.ds(0, units)]),
        (wu, lambda r: wgu.at[r, pl.ds(units, units)]),
        (wd, lambda r: wdn.at[:, r]),
    )
    for i, (src, dst) in enumerate(w_parts):
        pltpu.make_async_copy(src, dst(rows), wloc.at[i]).start()
        remote(src, dst(rows), wsend.at[i], wrecv.at[i], twin).start()

    right, left = here(k + 1), here(k - 1)

    def forward(t, zz, y, side):
        buf = (xb, zb)[t]
        return remote(
            buf.at[zz, y], buf.at[zz, y], fwd_send.at[t, side, zz, y], rx.at[t, zz, y], (left, right)[side]
        )

    halves = (yh, 1 - yh)

    def landed(t, zz, y):
        buf = (xb, zb)[t]
        remote(buf.at[zz, y], buf.at[zz, y], fwd_send.at[t, 0, zz, y], rx.at[t, zz, y], twin).wait_recv()

    def pass_on(t, zz, y, side):
        @pl.when(c > 0 if side == 0 else c < SHARES - 1)
        def _():
            forward(t, zz, y, side).start()

    def compute(zz):
        n_rows = 2 * CAP
        x = xb[zz].reshape(n_rows, width)
        gu = dot(x, wgu[...], 1, 0)
        back = dot(zb[zz].reshape(n_rows, width), wdn[...], 1, 1)
        gate, up = gu[:, :units], gu[:, units:]
        sig = jax.nn.sigmoid(gate)
        act = gate * sig
        hd[zz] = (act * up).astype(BF16)
        d_gate = (back * up * sig * (1.0 + gate * (1.0 - sig))).astype(BF16)
        d_up = (back * act).astype(BF16)
        d2[zz, :, :units] = d_gate
        d2[zz, :, units:] = d_up
        d = jnp.concatenate([d_gate, d_up], axis=1)
        chunk = 1024

        def part(n, _):
            cols = pl.ds(pl.multiple_of(n * chunk, chunk), chunk)
            pb[zz, :, :, cols] = dot(d, wgu[cols, :], 1, 1).astype(BF16).reshape(2, CAP, chunk)

        lax.fori_loop(0, width // chunk, part, None)

    def go_back(src, zz, y, side, at_end):
        slot = jnp.where(at_end, RING, zz) if side else zz
        return remote(
            src.at[zz, y], rb.at[slot, y], rsend.at[zz, y], rr.at[slot, y], (left, right)[side]
        )

    def go_home(src, zz, y):
        return remote(
            src.at[zz, y], f_out.at[mine], rsend.at[zz, y], fr.at[mine], here(y * RING + zz)
        )

    def add_part(zz, y):
        rb[zz, y] = (rb[zz, y].astype(F32) + pb[zz, y].astype(F32)).astype(BF16)

    def wait_back(slot, y):
        remote(rb.at[slot, y], rb.at[slot, y], rsend.at[0, 0], rr.at[slot, y], twin).wait_recv()

    last = STEPS - 1

    def z_moves(j):
        return (c - j, (j >= 1) & (j <= c + 2)), (c + j, (j >= 1) & (j <= 5 - c))

    def x_moves(j):
        p_left, p_right = j - LAG - 2 - c, last - j - c
        return (p_left, (p_left >= -2) & (p_left < c)), (p_right, (p_right <= 5) & (p_right > c))

    def back_moves(j):
        p_right, p_left = j - last + c, c + last - j
        return (p_right, (c < 3) & (p_right >= -2) & (p_right <= c)), (p_left, (c > 0) & (p_left <= 5) & (p_left >= c))

    def home_copy():
        return pltpu.make_async_copy(pb.at[z, yh], f_out.at[mine], fr.at[mine])

    def weight_cols(m):
        return pl.ds(pl.multiple_of(m * COLS, COLS), COLS)

    n_all = RING * 2 * CAP

    def grads_in(m, _):
        cols = weight_cols(m)
        xt = xb[:, :, :, cols].reshape(n_all, COLS)
        wgu[cols, :] = dot(xt, d2[...].reshape(n_all, 2 * units), 0, 0).astype(BF16)

    def grads_down(m, _):
        cols = weight_cols(m)
        zt = zb[:, :, :, cols].reshape(n_all, COLS)
        wdn[:, cols] = dot(hd[...].reshape(n_all, units), zt, 0, 0).astype(BF16)

    per_half = half // COLS
    send_in = remote(wgu.at[rows_far], g1, gsend.at[0], grecv.at[0], twin)
    send_down = remote(wdn.at[:, rows_far], g2, gsend.at[1], grecv.at[1], twin)

    def step(j, _):
        (z_l, z_in_left), (z_r, z_in_right) = z_moves(j)
        (x_l, x_in_left), (x_r, x_in_right) = x_moves(j)
        (b_r, from_right), (b_l, from_left) = back_moves(j)

        @pl.when(j == 0)
        def _():
            for y in halves:
                landed(1, z, y)
                pass_on(1, z, y, 0)
                pass_on(1, z, y, 1)

        @pl.when(j == X_ENTERS)
        def _():
            enter(0)

        for y in halves:
            for pos, valid, side in ((z_l, z_in_left, 1), (z_r, z_in_right, 0)):
                @pl.when(valid)
                def _():
                    landed(1, zof(pos), y)
                    pass_on(1, zof(pos), y, side)

        @pl.when(j == LAG)
        def _():
            for y in halves:
                landed(0, z, y)
            for i, (src, dst) in enumerate(w_parts):
                pltpu.make_async_copy(src, dst(rows), wloc.at[i]).wait()
                remote(src, dst(rows_far), wsend.at[i], wrecv.at[i], twin).wait_recv()

        for y in halves:
            for pos, valid, side in ((x_l, x_in_left, 1), (x_r, x_in_right, 0)):
                @pl.when(valid)
                def _():
                    landed(0, zof(pos), y)

                @pl.when(valid | (pos == c))
                def _():
                    pass_on(0, zof(pos), y, side)

        def side_step(side, _):
            pos = jnp.where(side == 2, c, jnp.where(side == 0, x_l, x_r))
            valid = ((side == 0) & x_in_left) | ((side == 1) & x_in_right) | ((side == 2) & (j == LAG))

            @pl.when(valid)
            def _():
                zz = zof(pos)
                compute(zz)

                @pl.when((side == 0) & (c == 3))
                def _():
                    for y in halves:
                        go_back(pb, zz, y, 0, False).start()

                @pl.when((side == 1) & (c == 0))
                def _():
                    for y in halves:
                        go_back(pb, zz, y, 1, pos == 1).start()

        lax.fori_loop(0, 3, side_step, None)

        for y in halves:
            @pl.when(from_right)
            def _():
                zz = zof(b_r)
                wait_back(zz, y)

                @pl.when(b_r < c)
                def _():
                    add_part(zz, y)

                    @pl.when(c > 0)
                    def _():
                        go_back(rb, zz, y, 0, False).start()

                    @pl.when(c == 0)
                    def _():
                        go_home(rb, zz, y).start()

            @pl.when(from_left)
            def _():
                zz = zof(b_l)

                @pl.when(b_l == c)
                def _():
                    wait_back(RING, y)

                @pl.when(b_l > c)
                def _():
                    wait_back(zz, y)
                    add_part(zz, y)

                    @pl.when(c < 3)
                    def _():
                        go_back(rb, zz, y, 1, b_l == c + 1).start()

                    @pl.when(c == 3)
                    def _():
                        go_home(rb, zz, y).start()

        @pl.when(j == last)
        def _():
            for y in (1 - yh, yh):
                @pl.when(c == 0)
                def _():
                    pb[z, y] = (pb[z, y].astype(F32) + rb[z, y].astype(F32)).astype(BF16)

                @pl.when(c == 3)
                def _():
                    pb[z, y] = (pb[z, y].astype(F32) + rb[RING, y].astype(F32)).astype(BF16)

                @pl.when((c > 0) & (c < 3))
                def _():
                    total = pb[z, y].astype(F32) + rb[z, y].astype(F32)
                    pb[z, y] = (total + rb[RING, y].astype(F32)).astype(BF16)

                @pl.when(y != yh)
                def _():
                    go_home(pb, z, y).start()

            home_copy().start()

        @pl.when(j == last - 1)
        def _():
            lax.fori_loop(other * per_half, (other + 1) * per_half, grads_in, None)
            send_in.start()

    lax.fori_loop(0, STEPS, step, None)
    lax.fori_loop(other * per_half, (other + 1) * per_half, grads_down, None)
    send_down.start()
    lax.fori_loop(rep * per_half, (rep + 1) * per_half, grads_in, None)
    lax.fori_loop(rep * per_half, (rep + 1) * per_half, grads_down, None)

    piece = 512

    send_in.wait_recv()

    def add_in(m, _):
        at = pl.ds(pl.multiple_of(m * piece, piece), piece)
        own = wgu[pl.ds(pl.multiple_of(rep * half + m * piece, piece), piece), :]
        g1[at, :] = (g1[at, :].astype(F32) + own.astype(F32)).astype(BF16)

    lax.fori_loop(0, half // piece, add_in, None)
    outs = [
        pltpu.make_async_copy(g1.at[:, pl.ds(0, units)], gg_out, gloc.at[0]),
        pltpu.make_async_copy(g1.at[:, pl.ds(units, units)], gu_out, gloc.at[1]),
        pltpu.make_async_copy(g2, gd_out, gloc.at[2]),
    ]
    outs[0].start()
    outs[1].start()
    send_down.wait_recv()

    def add_down(m, _):
        at = pl.ds(pl.multiple_of(m * piece, piece), piece)
        own = wdn[:, pl.ds(pl.multiple_of(rep * half + m * piece, piece), piece)]
        g2[:, at] = (g2[:, at].astype(F32) + own.astype(F32)).astype(BF16)

    lax.fori_loop(0, half // piece, add_down, None)
    outs[2].start()

    for e in range(EXPERTS):
        remote(f_out.at[e], f_out.at[e], rsend.at[0, 0], fr.at[e], twin).wait_recv()

    for e in range(EXPERTS):
        entry(e, 0).wait_send()

        @pl.when(mine != e)
        def _():
            entry(e, 1).wait_send()
    for i, (src, dst) in enumerate(w_parts):
        remote(src, dst(rows), wsend.at[i], wrecv.at[i], twin).wait_send()
    send_in.wait_send()
    send_down.wait_send()

    def drain(j, _):
        (z_l, z_in_left), (z_r, z_in_right) = z_moves(j)
        (x_l, x_in_left), (x_r, x_in_right) = x_moves(j)
        (b_r, from_right), (b_l, from_left) = back_moves(j)

        def sent(go, copy):
            @pl.when(go)
            def _():
                copy().wait_send()

        for y in halves:
            sent((z_in_left | (j == 0)) & (c < 3), lambda: forward(1, zof(z_l), y, 1))
            sent((z_in_right | (j == 0)) & (c > 0), lambda: forward(1, zof(z_r), y, 0))
            sent((x_in_left | (x_l == c)) & (c < 3), lambda: forward(0, zof(x_l), y, 1))
            sent((x_in_right | (x_r == c)) & (c > 0), lambda: forward(0, zof(x_r), y, 0))
            sent(x_in_left & (c == 3), lambda: go_back(pb, zof(x_l), y, 0, False))
            sent(x_in_right & (c == 0), lambda: go_back(pb, zof(x_r), y, 1, False))
            sent(from_right & (b_r < c) & (c > 0), lambda: go_back(rb, zof(b_r), y, 0, False))
            sent(from_left & (b_l > c) & (c < 3), lambda: go_back(rb, zof(b_l), y, 1, False))
            sent(from_right & (b_r < c) & (c == 0), lambda: go_home(rb, zof(b_r), y))
            sent(from_left & (b_l > c) & (c == 3), lambda: go_home(rb, zof(b_l), y))

    lax.fori_loop(0, STEPS, drain, None)
    go_home(pb, z, 1 - yh).wait_send()
    for out in outs:
        out.wait()


def placing_of(chosen):
    n_tok = chosen.shape[0]
    choose = chosen[:, None] == jnp.arange(EXPERTS, dtype=jnp.int32)[None, :]
    tok = jnp.arange(n_tok, dtype=jnp.int32)
    lower = (tok[:, None] > tok[None, :]).astype(BF16)
    before = dot(lower, choose.astype(BF16), 1, 0)
    slot = jnp.sum(jnp.where(choose, before, 0.0), axis=1).astype(jnp.int32)
    target = chosen * CAP + slot
    return (jnp.arange(EXPERTS * CAP, dtype=jnp.int32)[:, None] == target[None, :]).astype(BF16)


def body(saved_rows, grad_out, expert_ids, combine, w_gate, w_up, w_down):
    n_sec = lax.axis_size("section")
    chosen = expert_ids[0, :, 0]
    chosen_far = lax.ppermute(chosen, "section", [(i, n_sec - 1 - i) for i in range(n_sec)])
    width = saved_rows.shape[2]
    units = w_gate.shape[2]
    placing = placing_of(chosen)
    scaled = (combine[0] * grad_out[0].astype(F32)).astype(BF16)
    pz = dot(placing, scaled, 1, 0).astype(BF16).reshape(EXPERTS, CAP, width)
    px = dot(placing_of(chosen_far), saved_rows[0], 1, 0).astype(BF16)
    px = px.reshape(EXPERTS, CAP, width)
    half = width // 2
    dma = pltpu.SemaphoreType.DMA
    outs = pl.pallas_call(
        kernel,
        out_shape=(
            jax.ShapeDtypeStruct((EXPERTS, CAP, width), BF16),
            jax.ShapeDtypeStruct((half, units), BF16),
            jax.ShapeDtypeStruct((half, units), BF16),
            jax.ShapeDtypeStruct((units, half), BF16),
        ),
        in_specs=[pl.BlockSpec(memory_space=pl.ANY)] * 5,
        out_specs=[pl.BlockSpec(memory_space=pl.ANY)] * 4,
        scratch_shapes=[
            pltpu.VMEM((RING, 2, CAP, width), BF16),
            pltpu.VMEM((RING, 2, CAP, width), BF16),
            pltpu.VMEM((width, 2 * units), BF16),
            pltpu.VMEM((units, width), BF16),
            pltpu.VMEM((RING, 2, CAP, width), BF16),
            pltpu.VMEM((RING + 1, 2, CAP, width), BF16),
            pltpu.VMEM((RING, 2 * CAP, 2 * units), BF16),
            pltpu.VMEM((RING, 2 * CAP, units), BF16),
            pltpu.VMEM((half, 2 * units), BF16),
            pltpu.VMEM((units, half), BF16),
            dma((2, RING, 2)),
            dma((2, EXPERTS)),
            dma((2, 2, RING, 2)),
            dma((RING + 1, 2)),
            dma((RING, 2)),
            dma((EXPERTS,)),
            dma((3,)),
            dma((3,)),
            dma((3,)),
            dma((2,)),
            dma((2,)),
            dma((3,)),
        ],
        compiler_params=pltpu.CompilerParams(
            has_side_effects=True, vmem_limit_bytes=60 * 1024 * 1024
        ),
    )(px, pz, w_gate[0], w_up[0], w_down[0])
    merged, grad_gate, grad_up, grad_down = outs
    grad_in = dot(placing, merged.reshape(EXPERTS * CAP, width), 0, 0).astype(BF16)
    return grad_in[None], grad_gate[None], grad_up[None], grad_down[None]


def solution(mesh):
    return jax.shard_map(
        body,
        mesh=mesh,
        in_specs=(
            P("section", ("expert", "dp"), None),
            P("section", ("expert", "dp"), None),
            P("section", ("expert", "dp"), None),
            P("section", ("expert", "dp"), None),
            P("section", "dp", "expert"),
            P("section", "dp", "expert"),
            P("section", "expert", "dp"),
        ),
        out_specs=(
            P("section", ("expert", "dp"), None),
            P("section", "dp", "expert"),
            P("section", "dp", "expert"),
            P("section", "expert", "dp"),
        ),
        check_vma=False,
    )
```

```python
import functools

import jax
import jax.numpy as jnp
from jax import lax
from jax.experimental import pallas as pl
from jax.experimental.pallas import tpu as pltpu
from jax.sharding import PartitionSpec as P

EXPERTS = 4
CAP = 48
SHARES = 4
RING = 8
STEPS = 12
LAG = 3
COLS = 256
MESH = pl.DeviceIdType.MESH
F32 = jnp.float32
BF16 = jnp.bfloat16


def dot(a, b, dim_a, dim_b):
    return lax.dot_general(a, b, (((dim_a,), (dim_b,)), ((), ())), preferred_element_type=F32)


def slots_of(chosen):
    n_tok = chosen.shape[1]
    experts = lax.broadcasted_iota(jnp.int32, (8, n_tok), 0)
    choose = jnp.where(experts == chosen, 1.0, 0.0)
    earlier = lax.broadcasted_iota(jnp.int32, (n_tok, n_tok), 0) < lax.broadcasted_iota(
        jnp.int32, (n_tok, n_tok), 1
    )
    before = dot(choose.astype(BF16), jnp.where(earlier, 1.0, 0.0).astype(BF16), 1, 0)
    slot = jnp.sum(choose * before, axis=0, keepdims=True).astype(jnp.int32)
    return jnp.broadcast_to(chosen * CAP + slot, (8, n_tok))


def places(row):
    ids = lax.broadcasted_iota(jnp.int32, (EXPERTS * CAP, row.shape[1]), 0)
    return jnp.where(ids == row, 1.0, 0.0).astype(BF16)


def kernel(
    rows_in, rows_out, weight, chosen, wg, wu, wd,
    f_out, gg_out, gu_out, gd_out,
    px, pz, target, far_target, xb, zb, wgu, wdn, pb, rb, d2, hd, g1, g2,
    tsem, rx, ent_send, fwd_send, rr, rsend, fr, wrecv, wsend, wloc, grecv, gsend, gloc,
):
    sec, k, rep = lax.axis_index("section"), lax.axis_index("expert"), lax.axis_index("dp")
    mirror = lax.axis_size("section") - 1 - sec
    yh, z = k // RING, k % RING
    seg, c = z // SHARES, z % SHARES
    mine = 2 * yh + seg
    other = 1 - rep
    width = xb.shape[-1]
    half = width // 2
    units = hd.shape[-1]

    def zof(pos):
        return (SHARES * seg + pos + RING) % RING

    def here(expert):
        return (sec, expert, rep)

    twin = (sec, k, other)

    def remote(src, dst, send, recv, dev):
        return pltpu.make_async_remote_copy(
            src_ref=src, dst_ref=dst, send_sem=send, recv_sem=recv, device_id=dev, device_id_type=MESH
        )

    def entry(e, t):
        ye, te = e // 2, e % 2
        far = jnp.where(c < 2, SHARES - 1, 0)
        z_in = jnp.where(seg == te, z, te * SHARES + far)
        src, buf, s = ((px, xb, mirror), (pz, zb, sec))[t]
        return remote(
            src.at[e], buf.at[z, yh], ent_send.at[t, e], rx.at[t, z, yh], (s, ye * RING + z_in, rep)
        )

    def own_copy(e):
        return pltpu.make_async_copy(pz.at[e], zb.at[z, yh], rx.at[1, z, yh])

    def enter(t):
        for away in (False, True):
            for e in range(EXPERTS):
                go = (e % 2 != seg) if away else (e % 2 == seg)

                @pl.when(go if t == 0 else go & (mine != e))
                def _():
                    entry(e, t).start()

    bar = pltpu.get_barrier_semaphore()

    def greet(*dev):
        pl.semaphore_signal(bar, inc=1, device_id=dev, device_id_type=MESH)

    z_far = (1 - seg) * SHARES + jnp.where(c < 2, SHARES - 1, 0)
    step_far = jnp.where(c == 0, RING - 1, 1)
    at_end = (c == 0) | (c == SHARES - 1)
    greet(*twin)
    greet(sec, (1 - yh) * RING + z, rep)
    for ye in range(2):
        greet(sec, ye * RING + z_far, rep)
        greet(mirror, ye * RING + z, rep)
        greet(mirror, ye * RING + z_far, rep)

        @pl.when(at_end)
        def _():
            z_two = (z + 2 * step_far) % RING
            greet(sec, ye * RING + z_two, rep)
            greet(mirror, ye * RING + z_two, rep)

    @pl.when(c > 0)
    def _():
        greet(*here(k - 1))

    @pl.when(c < SHARES - 1)
    def _():
        greet(*here(k + 1))

    def pack(out, row, src, scale):
        placing = places(row)
        factor = None
        if scale is not None:
            factor = jnp.sum(placing.astype(F32) * scale, axis=1, keepdims=True)
        chunk = 1024

        def one(n, _):
            cols = pl.ds(pl.multiple_of(n * chunk, chunk), chunk)
            got = dot(placing, src[:, cols], 1, 0)
            if factor is not None:
                got = factor * got
            out[:, :, cols] = got.astype(BF16).reshape(EXPERTS, CAP, chunk)

        lax.fori_loop(0, width // chunk, one, None)

    target[...] = slots_of(chosen[...])
    pack(pz, target[0:1, :], rows_out, weight[...])
    pl.semaphore_wait(bar, jnp.where(at_end, 13, 10))

    for e in range(EXPERTS):
        @pl.when(mine == e)
        def _():
            own_copy(e).start()
    send_target = remote(target, far_target, tsem.at[0], tsem.at[1], (mirror, k, rep))
    send_target.start()
    enter(1)

    rows = pl.ds(pl.multiple_of(rep * half, half), half)
    rows_far = pl.ds(pl.multiple_of(other * half, half), half)
    w_parts = (
        (wg, lambda r: wgu.at[r, pl.ds(0, units)]),
        (wu, lambda r: wgu.at[r, pl.ds(units, units)]),
        (wd, lambda r: wdn.at[:, r]),
    )
    for i, (src, dst) in enumerate(w_parts):
        pltpu.make_async_copy(src, dst(rows), wloc.at[i]).start()
        remote(src, dst(rows), wsend.at[i], wrecv.at[i], twin).start()

    send_target.wait_recv()
    pack(px, far_target[0:1, :], rows_in, None)
    enter(0)

    right, left = here(k + 1), here(k - 1)

    def forward(t, zz, y, side):
        buf = (xb, zb)[t]
        return remote(
            buf.at[zz, y], buf.at[zz, y], fwd_send.at[t, side, zz, y], rx.at[t, zz, y], (left, right)[side]
        )

    halves = (yh, 1 - yh)
    backward = (1 - yh, yh)

    def landed(t, zz, y):
        buf = (xb, zb)[t]
        remote(buf.at[zz, y], buf.at[zz, y], fwd_send.at[t, 0, zz, y], rx.at[t, zz, y], twin).wait_recv()

    def pass_on(t, zz, y, side):
        @pl.when(c > 0 if side == 0 else c < SHARES - 1)
        def _():
            forward(t, zz, y, side).start()

    def compute(zz):
        n_rows = 2 * CAP
        x = xb[zz].reshape(n_rows, width)
        gu = dot(x, wgu[...], 1, 0)
        back = dot(zb[zz].reshape(n_rows, width), wdn[...], 1, 1)
        gate, up = gu[:, :units], gu[:, units:]
        sig = jax.nn.sigmoid(gate)
        act = gate * sig
        hd[zz] = (act * up).astype(BF16)
        d_gate = (back * up * sig * (1.0 + gate * (1.0 - sig))).astype(BF16)
        d_up = (back * act).astype(BF16)
        d2[zz, :, :units] = d_gate
        d2[zz, :, units:] = d_up
        d = jnp.concatenate([d_gate, d_up], axis=1)
        chunk = 1024

        def part(n, _):
            cols = pl.ds(pl.multiple_of(n * chunk, chunk), chunk)
            pb[zz, :, :, cols] = dot(d, wgu[cols, :], 1, 1).astype(BF16).reshape(2, CAP, chunk)

        lax.fori_loop(0, width // chunk, part, None)

    def go_back(src, zz, y, side, at_end):
        slot = jnp.where(at_end, RING, zz) if side else zz
        return remote(
            src.at[zz, y], rb.at[slot, y], rsend.at[zz, y], rr.at[slot, y], (left, right)[side]
        )

    def go_home(src, zz, y):
        return remote(
            src.at[zz, y], f_out.at[mine], rsend.at[zz, y], fr.at[mine], here(y * RING + zz)
        )

    def add_part(zz, y):
        rb[zz, y] = (rb[zz, y].astype(F32) + pb[zz, y].astype(F32)).astype(BF16)

    def wait_back(slot, y):
        remote(rb.at[slot, y], rb.at[slot, y], rsend.at[0, 0], rr.at[slot, y], twin).wait_recv()

    last = STEPS - 1

    def z_moves(j):
        return (c - j, (j >= 1) & (j <= c + 2)), (c + j, (j >= 1) & (j <= 5 - c))

    def x_moves(j):
        p_left, p_right = j - LAG - 2 - c, last - j - c
        return (p_left, (p_left >= -2) & (p_left < c)), (p_right, (p_right <= 5) & (p_right > c))

    def back_moves(j):
        p_right, p_left = j - last + c, c + last - j
        return (p_right, (c < 3) & (p_right >= -2) & (p_right <= c)), (p_left, (c > 0) & (p_left <= 5) & (p_left >= c))

    def home_copy():
        return pltpu.make_async_copy(pb.at[z, yh], f_out.at[mine], fr.at[mine])

    def weight_cols(m):
        return pl.ds(pl.multiple_of(m * COLS, COLS), COLS)

    n_all = RING * 2 * CAP

    def grads_in(m, _):
        cols = weight_cols(m)
        xt = xb[:, :, :, cols].reshape(n_all, COLS)
        wgu[cols, :] = dot(xt, d2[...].reshape(n_all, 2 * units), 0, 0).astype(BF16)

    def grads_down(m, _):
        cols = weight_cols(m)
        zt = zb[:, :, :, cols].reshape(n_all, COLS)
        wdn[:, cols] = dot(hd[...].reshape(n_all, units), zt, 0, 0).astype(BF16)

    per_half = half // COLS
    send_in = remote(wgu.at[rows_far], g1, gsend.at[0], grecv.at[0], twin)
    send_down = remote(wdn.at[:, rows_far], g2, gsend.at[1], grecv.at[1], twin)

    def step(j, _):
        (z_l, z_in_left), (z_r, z_in_right) = z_moves(j)
        (x_l, x_in_left), (x_r, x_in_right) = x_moves(j)
        (b_r, from_right), (b_l, from_left) = back_moves(j)

        @pl.when(j == 0)
        def _():
            for y in halves:
                landed(1, z, y)
                pass_on(1, z, y, 0)
                pass_on(1, z, y, 1)

        for y in halves:
            for pos, valid, side in ((z_l, z_in_left, 1), (z_r, z_in_right, 0)):
                @pl.when(valid)
                def _():
                    landed(1, zof(pos), y)
                    pass_on(1, zof(pos), y, side)

        @pl.when(j == LAG)
        def _():
            for y in halves:
                landed(0, z, y)
            for i, (src, dst) in enumerate(w_parts):
                pltpu.make_async_copy(src, dst(rows), wloc.at[i]).wait()
                remote(src, dst(rows_far), wsend.at[i], wrecv.at[i], twin).wait_recv()

        for y in halves:
            for pos, valid, side in ((x_l, x_in_left, 1), (x_r, x_in_right, 0)):
                @pl.when(valid)
                def _():
                    landed(0, zof(pos), y)

                @pl.when(valid | (pos == c))
                def _():
                    pass_on(0, zof(pos), y, side)

        def side_step(side, _):
            pos = jnp.where(side == 2, c, jnp.where(side == 0, x_l, x_r))
            valid = ((side == 0) & x_in_left) | ((side == 1) & x_in_right) | ((side == 2) & (j == LAG))

            @pl.when(valid)
            def _():
                zz = zof(pos)
                compute(zz)

                @pl.when((side == 0) & (c == 3))
                def _():
                    for y in backward:
                        go_back(pb, zz, y, 0, False).start()

                @pl.when((side == 1) & (c == 0))
                def _():
                    for y in backward:
                        go_back(pb, zz, y, 1, pos == 1).start()

        lax.fori_loop(0, 3, side_step, None)

        for y in backward:
            @pl.when(from_right)
            def _():
                zz = zof(b_r)
                wait_back(zz, y)

                @pl.when(b_r < c)
                def _():
                    add_part(zz, y)

                    @pl.when(c > 0)
                    def _():
                        go_back(rb, zz, y, 0, False).start()

                    @pl.when(c == 0)
                    def _():
                        go_home(rb, zz, y).start()

            @pl.when(from_left)
            def _():
                zz = zof(b_l)

                @pl.when(b_l == c)
                def _():
                    wait_back(RING, y)

                @pl.when(b_l > c)
                def _():
                    wait_back(zz, y)
                    add_part(zz, y)

                    @pl.when(c < 3)
                    def _():
                        go_back(rb, zz, y, 1, b_l == c + 1).start()

                    @pl.when(c == 3)
                    def _():
                        go_home(rb, zz, y).start()

            @pl.when(j == last)
            def _():
                @pl.when(c == 0)
                def _():
                    pb[z, y] = (pb[z, y].astype(F32) + rb[z, y].astype(F32)).astype(BF16)

                @pl.when(c == 3)
                def _():
                    pb[z, y] = (pb[z, y].astype(F32) + rb[RING, y].astype(F32)).astype(BF16)

                @pl.when((c > 0) & (c < 3))
                def _():
                    total = pb[z, y].astype(F32) + rb[z, y].astype(F32)
                    pb[z, y] = (total + rb[RING, y].astype(F32)).astype(BF16)

                if y is yh:
                    home_copy().start()
                else:
                    go_home(pb, z, y).start()

        @pl.when(j == last - 1)
        def _():
            lax.fori_loop(other * per_half, (other + 1) * per_half, grads_in, None)
            send_in.start()
            lax.fori_loop(other * per_half, (other + 1) * per_half, grads_down, None)
            send_down.start()
            lax.fori_loop(rep * per_half, (rep + 1) * per_half, grads_in, None)
            lax.fori_loop(rep * per_half, (rep + 1) * per_half, grads_down, None)

    lax.fori_loop(0, STEPS, step, None)

    piece = 512

    send_in.wait_recv()

    def add_in(m, _):
        at = pl.ds(pl.multiple_of(m * piece, piece), piece)
        own = wgu[pl.ds(pl.multiple_of(rep * half + m * piece, piece), piece), :]
        g1[at, :] = (g1[at, :].astype(F32) + own.astype(F32)).astype(BF16)

    lax.fori_loop(0, half // piece, add_in, None)
    outs = [
        pltpu.make_async_copy(g1.at[:, pl.ds(0, units)], gg_out, gloc.at[0]),
        pltpu.make_async_copy(g1.at[:, pl.ds(units, units)], gu_out, gloc.at[1]),
        pltpu.make_async_copy(g2, gd_out, gloc.at[2]),
    ]
    outs[0].start()
    outs[1].start()
    send_down.wait_recv()

    def add_down(m, _):
        at = pl.ds(pl.multiple_of(m * piece, piece), piece)
        own = wdn[:, pl.ds(pl.multiple_of(rep * half + m * piece, piece), piece)]
        g2[:, at] = (g2[:, at].astype(F32) + own.astype(F32)).astype(BF16)

    lax.fori_loop(0, half // piece, add_down, None)
    outs[2].start()

    for e in range(EXPERTS):
        remote(f_out.at[e], f_out.at[e], rsend.at[0, 0], fr.at[e], twin).wait_recv()

    for e in range(EXPERTS):
        entry(e, 0).wait_send()

        @pl.when(mine != e)
        def _():
            entry(e, 1).wait_send()
    for i, (src, dst) in enumerate(w_parts):
        remote(src, dst(rows), wsend.at[i], wrecv.at[i], twin).wait_send()
    send_target.wait_send()
    send_in.wait_send()
    send_down.wait_send()

    def drain(j, _):
        (z_l, z_in_left), (z_r, z_in_right) = z_moves(j)
        (x_l, x_in_left), (x_r, x_in_right) = x_moves(j)
        (b_r, from_right), (b_l, from_left) = back_moves(j)

        def sent(go, copy):
            @pl.when(go)
            def _():
                copy().wait_send()

        for y in halves:
            sent((z_in_left | (j == 0)) & (c < 3), lambda: forward(1, zof(z_l), y, 1))
            sent((z_in_right | (j == 0)) & (c > 0), lambda: forward(1, zof(z_r), y, 0))
            sent((x_in_left | (x_l == c)) & (c < 3), lambda: forward(0, zof(x_l), y, 1))
            sent((x_in_right | (x_r == c)) & (c > 0), lambda: forward(0, zof(x_r), y, 0))
            sent(x_in_left & (c == 3), lambda: go_back(pb, zof(x_l), y, 0, False))
            sent(x_in_right & (c == 0), lambda: go_back(pb, zof(x_r), y, 1, False))
            sent(from_right & (b_r < c) & (c > 0), lambda: go_back(rb, zof(b_r), y, 0, False))
            sent(from_left & (b_l > c) & (c < 3), lambda: go_back(rb, zof(b_l), y, 1, False))
            sent(from_right & (b_r < c) & (c == 0), lambda: go_home(rb, zof(b_r), y))
            sent(from_left & (b_l > c) & (c == 3), lambda: go_home(rb, zof(b_l), y))

    lax.fori_loop(0, STEPS, drain, None)
    go_home(pb, z, 1 - yh).wait_send()
    for out in outs:
        out.wait()


def finish_kernel(merged, chosen, gg, gu, gd, gi_out, gg_out, gu_out, gd_out):
    placing = places(slots_of(chosen[...])[0:1, :])
    gi_out[...] = dot(placing, merged[...], 0, 0).astype(BF16)
    gg_out[...] = gg[...]
    gu_out[...] = gu[...]
    gd_out[...] = gd[...]


def body(saved_rows, grad_out, expert_ids, combine, w_gate, w_up, w_down):
    tokens, width = saved_rows.shape[1:]
    units = w_gate.shape[2]
    half = width // 2
    chosen = expert_ids.reshape(1, tokens)
    weight = combine.reshape(1, tokens)
    dma = pltpu.SemaphoreType.DMA
    anywhere = pl.BlockSpec(memory_space=pl.ANY)
    in_vmem = pl.BlockSpec(memory_space=pltpu.VMEM)
    grad_shapes = (
        jax.ShapeDtypeStruct((half, units), BF16),
        jax.ShapeDtypeStruct((half, units), BF16),
        jax.ShapeDtypeStruct((units, half), BF16),
    )
    merged, *grads = pl.pallas_call(
        kernel,
        out_shape=(jax.ShapeDtypeStruct((EXPERTS, CAP, width), BF16),) + grad_shapes,
        in_specs=[in_vmem] * 4 + [anywhere] * 3,
        out_specs=[anywhere] * 4,
        scratch_shapes=[
            pltpu.VMEM((EXPERTS, CAP, width), BF16),
            pltpu.VMEM((EXPERTS, CAP, width), BF16),
            pltpu.VMEM((8, tokens), jnp.int32),
            pltpu.VMEM((8, tokens), jnp.int32),
            pltpu.VMEM((RING, 2, CAP, width), BF16),
            pltpu.VMEM((RING, 2, CAP, width), BF16),
            pltpu.VMEM((width, 2 * units), BF16),
            pltpu.VMEM((units, width), BF16),
            pltpu.VMEM((RING, 2, CAP, width), BF16),
            pltpu.VMEM((RING + 1, 2, CAP, width), BF16),
            pltpu.VMEM((RING, 2 * CAP, 2 * units), BF16),
            pltpu.VMEM((RING, 2 * CAP, units), BF16),
            pltpu.VMEM((half, 2 * units), BF16),
            pltpu.VMEM((units, half), BF16),
            dma((2,)),
            dma((2, RING, 2)),
            dma((2, EXPERTS)),
            dma((2, 2, RING, 2)),
            dma((RING + 1, 2)),
            dma((RING, 2)),
            dma((EXPERTS,)),
            dma((3,)),
            dma((3,)),
            dma((3,)),
            dma((2,)),
            dma((2,)),
            dma((3,)),
        ],
        compiler_params=pltpu.CompilerParams(
            collective_id=0, has_side_effects=True, vmem_limit_bytes=60 * 1024 * 1024
        ),
    )(saved_rows[0], grad_out[0], weight, chosen, w_gate[0], w_up[0], w_down[0])
    steps = 2
    slots = EXPERTS * CAP
    row_spec = pl.BlockSpec((half // steps, units), lambda i: (i, 0))
    grad_specs = [row_spec, row_spec, pl.BlockSpec((units // steps, half), lambda i: (i, 0))]
    grad_in, *grads = pl.pallas_call(
        finish_kernel,
        grid=(steps,),
        out_shape=(jax.ShapeDtypeStruct((tokens, width), BF16),) + grad_shapes,
        in_specs=[
            pl.BlockSpec((slots, width // steps), lambda i: (0, i)),
            pl.BlockSpec((1, tokens), lambda i: (0, 0)),
        ]
        + grad_specs,
        out_specs=[pl.BlockSpec((tokens, width // steps), lambda i: (0, i))] + grad_specs,
        compiler_params=pltpu.CompilerParams(vmem_limit_bytes=60 * 1024 * 1024),
    )(merged.reshape(slots, width), chosen, *grads)
    return grad_in[None], *(grad[None] for grad in grads)


def solution(mesh):
    return jax.shard_map(
        body,
        mesh=mesh,
        in_specs=(
            P("section", ("expert", "dp"), None),
            P("section", ("expert", "dp"), None),
            P("section", ("expert", "dp"), None),
            P("section", ("expert", "dp"), None),
            P("section", "dp", "expert"),
            P("section", "dp", "expert"),
            P("section", "expert", "dp"),
        ),
        out_specs=(
            P("section", ("expert", "dp"), None),
            P("section", "dp", "expert"),
            P("section", "dp", "expert"),
            P("section", "expert", "dp"),
        ),
        check_vma=False,
    )
```

```python
import functools

import jax
import jax.numpy as jnp
from jax import lax
from jax.experimental import pallas as pl
from jax.experimental.pallas import tpu as pltpu
from jax.sharding import PartitionSpec as P

EXPERTS = 4
CAP = 48
SHARES = 4
RING = 8
LAG = 3
X_LAST = LAG + 8
STEPS = X_LAST + 2
COLS = 256
MESH = pl.DeviceIdType.MESH
F32 = jnp.float32
BF16 = jnp.bfloat16


def dot(a, b, dim_a, dim_b):
    return lax.dot_general(a, b, (((dim_a,), (dim_b,)), ((), ())), preferred_element_type=F32)


def slots_of(chosen):
    n_tok = chosen.shape[1]
    experts = lax.broadcasted_iota(jnp.int32, (8, n_tok), 0)
    choose = jnp.where(experts == chosen, 1.0, 0.0)
    earlier = lax.broadcasted_iota(jnp.int32, (n_tok, n_tok), 0) < lax.broadcasted_iota(
        jnp.int32, (n_tok, n_tok), 1
    )
    before = dot(choose.astype(BF16), jnp.where(earlier, 1.0, 0.0).astype(BF16), 1, 0)
    slot = jnp.sum(choose * before, axis=0, keepdims=True).astype(jnp.int32)
    return jnp.broadcast_to(chosen * CAP + slot, (8, n_tok))


def places(row, slots=EXPERTS * CAP):
    ids = lax.broadcasted_iota(jnp.int32, (slots, row.shape[1]), 0)
    return jnp.where(ids == row, 1.0, 0.0).astype(BF16)


def kernel(
    rows_in, rows_out, weight, chosen, wg, wu, wd,
    f_out, gg_out, gu_out, gd_out,
    px, pz, pn, raw, target, far_target, near_target, xb, zb, wgu, wdn, pb, rb, d2, hd, g1, g2,
    tsem, raw_send, raw_recv, rx, ent_send, fwd_send, rr, rsend, fr, wrecv, wsend, wloc, grecv, gsend, gloc,
):
    sec, k, rep = lax.axis_index("section"), lax.axis_index("expert"), lax.axis_index("dp")
    mirror = lax.axis_size("section") - 1 - sec
    yh, z = k // RING, k % RING
    seg, c = z // SHARES, z % SHARES
    mine = 2 * yh + seg
    other = 1 - rep
    width = xb.shape[-1]
    half = width // 2
    units = hd.shape[-1]

    def zof(pos):
        return (SHARES * seg + pos + RING) % RING

    def here(expert):
        return (sec, expert, rep)

    twin = (sec, k, other)

    def remote(src, dst, send, recv, dev):
        return pltpu.make_async_remote_copy(
            src_ref=src, dst_ref=dst, send_sem=send, recv_sem=recv, device_id=dev, device_id_type=MESH
        )

    pair = z + 1 - 2 * (z % 2)
    z_far = (1 - seg) * SHARES + jnp.where(c < 2, SHARES - 1, 0)
    at_end = (c == 0) | (c == SHARES - 1)
    inner = (c > 0) & (c < SHARES - 1)

    def entry(e, t, proxy):
        ye, te = e // 2, e % 2
        z_in = jnp.where(seg == te, z, z_far)
        src = pn.at[t] if proxy else (px, pz)[t]
        to = sec if proxy or t == 1 else mirror
        slot = pair if proxy else z
        return remote(
            src.at[e], (xb, zb)[t].at[slot, yh], ent_send.at[proxy, t, e], rx.at[t, slot, yh],
            (to, ye * RING + z_in, rep),
        )

    def entries(t, proxy, act):
        for away in (False, True):
            for e in range(EXPERTS):
                go = (seg != e % 2) & at_end if away else seg == e % 2

                @pl.when(go if t == 0 and not proxy else go & (mine != e))
                def _():
                    act(entry(e, t, proxy))

    def own_copy(e, t, proxy):
        slot = pair if proxy else z
        src = pn.at[t] if proxy else pz
        return pltpu.make_async_copy(src.at[e], (xb, zb)[t].at[slot, yh], rx.at[t, slot, yh])

    def keep(t, proxy):
        for e in range(EXPERTS):
            @pl.when(mine == e)
            def _():
                own_copy(e, t, proxy).start()

    bar = pltpu.get_barrier_semaphore()

    def greet(*dev):
        pl.semaphore_signal(bar, inc=1, device_id=dev, device_id_type=MESH)

    step_far = jnp.where(c == 0, RING - 1, 1)
    greet(*twin)
    greet(sec, (1 - yh) * RING + z, rep)
    greet(mirror, yh * RING + pair, rep)
    for ye in range(2):
        greet(sec, ye * RING + z_far, rep)
        greet(mirror, ye * RING + z, rep)

        @pl.when(at_end)
        def _():
            greet(sec, ye * RING + (z + 2 * step_far) % RING, rep)
            greet(mirror, ye * RING + z_far, rep)

    @pl.when(c > 0)
    def _():
        greet(*here(k - 1))

    @pl.when(c < SHARES - 1)
    def _():
        greet(*here(k + 1))

    def pack(out, placing, src, scale):
        factor = None
        if scale is not None:
            factor = jnp.sum(placing.astype(F32) * scale, axis=1, keepdims=True)
        chunk = 1024

        def one(n, _):
            cols = pl.ds(pl.multiple_of(n * chunk, chunk), chunk)
            got = dot(placing, src[:, cols], 1, 0)
            if factor is not None:
                got = factor * got
            got = got.astype(BF16)
            out[..., cols] = got.reshape(out.shape[:-1] + (chunk,))

        lax.fori_loop(0, width // chunk, one, None)

    target[...] = slots_of(chosen[...])
    n_tok = raw.shape[1]

    @pl.when(inner)
    def _():
        tokens = lax.broadcasted_iota(jnp.int32, (1, n_tok), 1)
        pack(raw.at[1], places(tokens, n_tok), rows_out, weight[...])

    pack(pz, places(target[0:1, :]), rows_out, weight[...])
    pl.semaphore_wait(bar, jnp.where(at_end, 12, 9))

    near = here(yh * RING + pair)
    raw_copies = (
        remote(target, near_target, raw_send.at[0], raw_recv.at[0], near),
        remote(raw.at[1], raw.at[1], raw_send.at[1], raw_recv.at[1], near),
        remote(rows_in, raw.at[0], raw_send.at[2], raw_recv.at[2], (mirror, yh * RING + pair, rep)),
    )
    keep(1, 0)
    send_target = remote(target, far_target, tsem.at[0], tsem.at[1], (mirror, k, rep))
    send_target.start()

    @pl.when(inner)
    def _():
        raw_copies[0].start()
        raw_copies[1].start()

    entries(1, 0, lambda copy: copy.start())

    @pl.when(inner)
    def _():
        raw_copies[2].start()

    def enter_near(t):
        if t == 1:
            raw_copies[0].wait_recv()
        raw_copies[2 - t].wait_recv()
        pack(pn.at[t], places(near_target[0:1, :]), raw.at[t], None)
        keep(t, 1)
        entries(t, 1, lambda copy: copy.start())

    rows = pl.ds(pl.multiple_of(rep * half, half), half)
    rows_far = pl.ds(pl.multiple_of(other * half, half), half)
    w_parts = (
        (wg, lambda r: wgu.at[r, pl.ds(0, units)]),
        (wu, lambda r: wgu.at[r, pl.ds(units, units)]),
        (wd, lambda r: wdn.at[:, r]),
    )
    for i, (src, dst) in enumerate(w_parts):
        pltpu.make_async_copy(src, dst(rows), wloc.at[i]).start()
        remote(src, dst(rows), wsend.at[i], wrecv.at[i], twin).start()

    send_target.wait_recv()
    pack(px, places(far_target[0:1, :]), rows_in, None)
    entries(0, 0, lambda copy: copy.start())

    right, left = here(k + 1), here(k - 1)

    def forward(t, zz, y, side):
        buf = (xb, zb)[t]
        return remote(
            buf.at[zz, y], buf.at[zz, y], fwd_send.at[t, side, zz, y], rx.at[t, zz, y], (left, right)[side]
        )

    halves = (yh, 1 - yh)
    backward = (1 - yh, yh)

    def landed(t, zz, y):
        buf = (xb, zb)[t]
        remote(buf.at[zz, y], buf.at[zz, y], fwd_send.at[t, 0, zz, y], rx.at[t, zz, y], twin).wait_recv()

    onward = (c > 0, c < SHARES - 1)
    own_onward = (c >= 2, c <= 1)

    def compute(zz):
        n_rows = 2 * CAP
        x = xb[zz].reshape(n_rows, width)
        gu = dot(x, wgu[...], 1, 0)
        back = dot(zb[zz].reshape(n_rows, width), wdn[...], 1, 1)
        gate, up = gu[:, :units], gu[:, units:]
        sig = jax.nn.sigmoid(gate)
        act = gate * sig
        hd[zz] = (act * up).astype(BF16)
        d_gate = (back * up * sig * (1.0 + gate * (1.0 - sig))).astype(BF16)
        d_up = (back * act).astype(BF16)
        d2[zz, :, :units] = d_gate
        d2[zz, :, units:] = d_up
        d = jnp.concatenate([d_gate, d_up], axis=1)
        chunk = 1024

        def part(n, _):
            cols = pl.ds(pl.multiple_of(n * chunk, chunk), chunk)
            pb[zz, :, :, cols] = dot(d, wgu[cols, :], 1, 1).astype(BF16).reshape(2, CAP, chunk)

        lax.fori_loop(0, width // chunk, part, None)

    def go_back(src, zz, y, side, at_end):
        slot = jnp.where(at_end, RING, zz) if side else zz
        return remote(
            src.at[zz, y], rb.at[slot, y], rsend.at[zz, y], rr.at[slot, y], (left, right)[side]
        )

    def go_home(src, zz, y):
        return remote(
            src.at[zz, y], f_out.at[mine], rsend.at[zz, y], fr.at[mine], here(y * RING + zz)
        )

    def add_part(zz, y):
        rb[zz, y] = (rb[zz, y].astype(F32) + pb[zz, y].astype(F32)).astype(BF16)

    def wait_back(slot, y):
        remote(rb.at[slot, y], rb.at[slot, y], rsend.at[0, 0], rr.at[slot, y], twin).wait_recv()

    last = STEPS - 1

    def z_moves(j):
        return (c - j, (j >= 1) & (j <= c + 2)), (c + j, (j >= 1) & (j <= 5 - c))

    def x_moves(j):
        p_left, p_right = j - LAG - 2 - c, X_LAST - j - c
        return (p_left, (p_left >= -2) & (p_left < c)), (p_right, (p_right <= 5) & (p_right > c))

    def back_moves(j):
        p_right, p_left = j - last + c, c + last - j
        return (p_right, (c < 3) & (p_right >= -2) & (p_right <= c)), (p_left, (c > 0) & (p_left <= 5) & (p_left >= c))

    def home_copy():
        return pltpu.make_async_copy(pb.at[z, yh], f_out.at[mine], fr.at[mine])

    def weight_cols(m):
        return pl.ds(pl.multiple_of(m * COLS, COLS), COLS)

    n_all = RING * 2 * CAP

    def grads_in(m, _):
        cols = weight_cols(m)
        xt = xb[:, :, :, cols].reshape(n_all, COLS)
        wgu[cols, :] = dot(xt, d2[...].reshape(n_all, 2 * units), 0, 0).astype(BF16)

    def grads_down(m, _):
        cols = weight_cols(m)
        zt = zb[:, :, :, cols].reshape(n_all, COLS)
        wdn[:, cols] = dot(hd[...].reshape(n_all, units), zt, 0, 0).astype(BF16)

    per_half = half // COLS
    send_in = remote(wgu.at[rows_far], g1, gsend.at[0], grecv.at[0], twin)
    send_down = remote(wdn.at[:, rows_far], g2, gsend.at[1], grecv.at[1], twin)

    def step(j, _):
        (z_l, z_in_left), (z_r, z_in_right) = z_moves(j)
        (x_l, x_in_left), (x_r, x_in_right) = x_moves(j)
        (b_r, from_right), (b_l, from_left) = back_moves(j)

        @pl.when(j == 0)
        def _():
            for y in halves:
                landed(1, z, y)
                for side in range(2):
                    @pl.when(own_onward[side])
                    def _():
                        forward(1, z, y, side).start()

        for y in halves:
            for pos, valid, side in ((z_l, z_in_left, 1), (z_r, z_in_right, 0)):
                @pl.when(valid & onward[side])
                def _():
                    landed(1, zof(pos), y)
                    forward(1, zof(pos), y, side).start()

        for t in (1, 0):
            @pl.when((j == 2 - t) & at_end)
            def _():
                enter_near(t)

        @pl.when(j == LAG)
        def _():
            for y in halves:
                landed(0, z, y)
            for i, (src, dst) in enumerate(w_parts):
                pltpu.make_async_copy(src, dst(rows), wloc.at[i]).wait()
                remote(src, dst(rows_far), wsend.at[i], wrecv.at[i], twin).wait_recv()

        for y in halves:
            for pos, valid, side in ((x_l, x_in_left, 1), (x_r, x_in_right, 0)):
                @pl.when(valid)
                def _():
                    landed(0, zof(pos), y)

                @pl.when((valid & onward[side]) | ((pos == c) & own_onward[side]))
                def _():
                    forward(0, zof(pos), y, side).start()

                @pl.when(valid & ~onward[side])
                def _():
                    landed(1, zof(pos), y)

        def side_step(side, _):
            pos = jnp.where(side == 2, c, jnp.where(side == 0, x_l, x_r))
            valid = ((side == 0) & x_in_left) | ((side == 1) & x_in_right) | ((side == 2) & (j == LAG))

            @pl.when(valid)
            def _():
                zz = zof(pos)
                compute(zz)

                @pl.when((side == 0) & (c == 3))
                def _():
                    for y in backward:
                        go_back(pb, zz, y, 0, False).start()

                @pl.when((side == 1) & (c == 0))
                def _():
                    for y in backward:
                        go_back(pb, zz, y, 1, pos == 1).start()

        lax.fori_loop(0, 3, side_step, None)

        for y in backward:
            @pl.when(from_right)
            def _():
                zz = zof(b_r)
                wait_back(zz, y)

                @pl.when(b_r < c)
                def _():
                    add_part(zz, y)

                    @pl.when(c > 0)
                    def _():
                        go_back(rb, zz, y, 0, False).start()

                    @pl.when(c == 0)
                    def _():
                        go_home(rb, zz, y).start()

            @pl.when(from_left)
            def _():
                zz = zof(b_l)

                @pl.when(b_l == c)
                def _():
                    wait_back(RING, y)

                @pl.when(b_l > c)
                def _():
                    wait_back(zz, y)
                    add_part(zz, y)

                    @pl.when(c < 3)
                    def _():
                        go_back(rb, zz, y, 1, b_l == c + 1).start()

                    @pl.when(c == 3)
                    def _():
                        go_home(rb, zz, y).start()

            @pl.when(j == last)
            def _():
                @pl.when(c == 0)
                def _():
                    pb[z, y] = (pb[z, y].astype(F32) + rb[z, y].astype(F32)).astype(BF16)

                @pl.when(c == 3)
                def _():
                    pb[z, y] = (pb[z, y].astype(F32) + rb[RING, y].astype(F32)).astype(BF16)

                @pl.when((c > 0) & (c < 3))
                def _():
                    total = pb[z, y].astype(F32) + rb[z, y].astype(F32)
                    pb[z, y] = (total + rb[RING, y].astype(F32)).astype(BF16)

                if y is yh:
                    home_copy().start()
                else:
                    go_home(pb, z, y).start()

        @pl.when(j == jnp.where(inner, X_LAST - 2, X_LAST - 1))
        def _():
            lax.fori_loop(other * per_half, (other + 1) * per_half, grads_in, None)
            send_in.start()

        @pl.when(j == jnp.where(inner, X_LAST - 2, X_LAST - 1))
        def _():
            lax.fori_loop(other * per_half, (other + 1) * per_half, grads_down, None)
            send_down.start()

        @pl.when(j == jnp.where(inner, X_LAST - 2, X_LAST - 1))
        def _():
            lax.fori_loop(rep * per_half, (rep + 1) * per_half, grads_in, None)

        @pl.when(j == jnp.where(inner, X_LAST - 2, X_LAST - 1))
        def _():
            lax.fori_loop(rep * per_half, (rep + 1) * per_half, grads_down, None)

    lax.fori_loop(0, STEPS, step, None)

    piece = 512

    send_in.wait_recv()

    def add_in(m, _):
        at = pl.ds(pl.multiple_of(m * piece, piece), piece)
        own = wgu[pl.ds(pl.multiple_of(rep * half + m * piece, piece), piece), :]
        g1[at, :] = (g1[at, :].astype(F32) + own.astype(F32)).astype(BF16)

    lax.fori_loop(0, half // piece, add_in, None)
    outs = [
        pltpu.make_async_copy(g1.at[:, pl.ds(0, units)], gg_out, gloc.at[0]),
        pltpu.make_async_copy(g1.at[:, pl.ds(units, units)], gu_out, gloc.at[1]),
        pltpu.make_async_copy(g2, gd_out, gloc.at[2]),
    ]
    outs[0].start()
    outs[1].start()
    send_down.wait_recv()

    def add_down(m, _):
        at = pl.ds(pl.multiple_of(m * piece, piece), piece)
        own = wdn[:, pl.ds(pl.multiple_of(rep * half + m * piece, piece), piece)]
        g2[:, at] = (g2[:, at].astype(F32) + own.astype(F32)).astype(BF16)

    lax.fori_loop(0, half // piece, add_down, None)
    outs[2].start()

    for e in range(EXPERTS):
        remote(f_out.at[e], f_out.at[e], rsend.at[0, 0], fr.at[e], twin).wait_recv()

    for t in range(2):
        entries(t, 0, lambda copy: copy.wait_send())

        @pl.when(at_end)
        def _():
            entries(t, 1, lambda copy: copy.wait_send())

    @pl.when(inner)
    def _():
        for copy in raw_copies:
            copy.wait_send()

    for i, (src, dst) in enumerate(w_parts):
        remote(src, dst(rows), wsend.at[i], wrecv.at[i], twin).wait_send()
    send_target.wait_send()
    send_in.wait_send()
    send_down.wait_send()

    def drain(j, _):
        (z_l, z_in_left), (z_r, z_in_right) = z_moves(j)
        (x_l, x_in_left), (x_r, x_in_right) = x_moves(j)
        (b_r, from_right), (b_l, from_left) = back_moves(j)

        def sent(go, copy):
            @pl.when(go)
            def _():
                copy().wait_send()

        for y in halves:
            sent((z_in_left & onward[1]) | ((j == 0) & own_onward[1]), lambda: forward(1, zof(z_l), y, 1))
            sent((z_in_right & onward[0]) | ((j == 0) & own_onward[0]), lambda: forward(1, zof(z_r), y, 0))
            sent((x_in_left & onward[1]) | ((x_l == c) & own_onward[1]), lambda: forward(0, zof(x_l), y, 1))
            sent((x_in_right & onward[0]) | ((x_r == c) & own_onward[0]), lambda: forward(0, zof(x_r), y, 0))
            sent(x_in_left & (c == 3), lambda: go_back(pb, zof(x_l), y, 0, False))
            sent(x_in_right & (c == 0), lambda: go_back(pb, zof(x_r), y, 1, False))
            sent(from_right & (b_r < c) & (c > 0), lambda: go_back(rb, zof(b_r), y, 0, False))
            sent(from_left & (b_l > c) & (c < 3), lambda: go_back(rb, zof(b_l), y, 1, False))
            sent(from_right & (b_r < c) & (c == 0), lambda: go_home(rb, zof(b_r), y))
            sent(from_left & (b_l > c) & (c == 3), lambda: go_home(rb, zof(b_l), y))

    lax.fori_loop(0, STEPS, drain, None)
    go_home(pb, z, 1 - yh).wait_send()
    for out in outs:
        out.wait()


def finish_kernel(merged, chosen, gg, gu, gd, gi_out, gg_out, gu_out, gd_out):
    placing = places(slots_of(chosen[...])[0:1, :])
    gi_out[...] = dot(placing, merged[...], 0, 0).astype(BF16)
    gg_out[...] = gg[...]
    gu_out[...] = gu[...]
    gd_out[...] = gd[...]


def body(saved_rows, grad_out, expert_ids, combine, w_gate, w_up, w_down):
    tokens, width = saved_rows.shape[1:]
    units = w_gate.shape[2]
    half = width // 2
    chosen = expert_ids.reshape(1, tokens)
    weight = combine.reshape(1, tokens)
    dma = pltpu.SemaphoreType.DMA
    anywhere = pl.BlockSpec(memory_space=pl.ANY)
    in_vmem = pl.BlockSpec(memory_space=pltpu.VMEM)
    grad_shapes = (
        jax.ShapeDtypeStruct((half, units), BF16),
        jax.ShapeDtypeStruct((half, units), BF16),
        jax.ShapeDtypeStruct((units, half), BF16),
    )
    merged, *grads = pl.pallas_call(
        kernel,
        out_shape=(jax.ShapeDtypeStruct((EXPERTS, CAP, width), BF16),) + grad_shapes,
        in_specs=[in_vmem] * 4 + [anywhere] * 3,
        out_specs=[anywhere] * 4,
        scratch_shapes=[
            pltpu.VMEM((EXPERTS, CAP, width), BF16),
            pltpu.VMEM((EXPERTS, CAP, width), BF16),
            pltpu.VMEM((2, EXPERTS, CAP, width), BF16),
            pltpu.VMEM((2, tokens, width), BF16),
            pltpu.VMEM((8, tokens), jnp.int32),
            pltpu.VMEM((8, tokens), jnp.int32),
            pltpu.VMEM((8, tokens), jnp.int32),
            pltpu.VMEM((RING, 2, CAP, width), BF16),
            pltpu.VMEM((RING, 2, CAP, width), BF16),
            pltpu.VMEM((width, 2 * units), BF16),
            pltpu.VMEM((units, width), BF16),
            pltpu.VMEM((RING, 2, CAP, width), BF16),
            pltpu.VMEM((RING + 1, 2, CAP, width), BF16),
            pltpu.VMEM((RING, 2 * CAP, 2 * units), BF16),
            pltpu.VMEM((RING, 2 * CAP, units), BF16),
            pltpu.VMEM((half, 2 * units), BF16),
            pltpu.VMEM((units, half), BF16),
            dma((2,)),
            dma((3,)),
            dma((3,)),
            dma((2, RING, 2)),
            dma((2, 2, EXPERTS)),
            dma((2, 2, RING, 2)),
            dma((RING + 1, 2)),
            dma((RING, 2)),
            dma((EXPERTS,)),
            dma((3,)),
            dma((3,)),
            dma((3,)),
            dma((2,)),
            dma((2,)),
            dma((3,)),
        ],
        compiler_params=pltpu.CompilerParams(
            collective_id=0, has_side_effects=True, vmem_limit_bytes=60 * 1024 * 1024
        ),
    )(saved_rows[0], grad_out[0], weight, chosen, w_gate[0], w_up[0], w_down[0])
    steps = 2
    slots = EXPERTS * CAP
    row_spec = pl.BlockSpec((half // steps, units), lambda i: (i, 0))
    grad_specs = [row_spec, row_spec, pl.BlockSpec((units // steps, half), lambda i: (i, 0))]
    grad_in, *grads = pl.pallas_call(
        finish_kernel,
        grid=(steps,),
        out_shape=(jax.ShapeDtypeStruct((tokens, width), BF16),) + grad_shapes,
        in_specs=[
            pl.BlockSpec((slots, width // steps), lambda i: (0, i)),
            pl.BlockSpec((1, tokens), lambda i: (0, 0)),
        ]
        + grad_specs,
        out_specs=[pl.BlockSpec((tokens, width // steps), lambda i: (0, i))] + grad_specs,
        compiler_params=pltpu.CompilerParams(vmem_limit_bytes=60 * 1024 * 1024),
    )(merged.reshape(slots, width), chosen, *grads)
    return grad_in[None], *(grad[None] for grad in grads)


def solution(mesh):
    return jax.shard_map(
        body,
        mesh=mesh,
        in_specs=(
            P("section", ("expert", "dp"), None),
            P("section", ("expert", "dp"), None),
            P("section", ("expert", "dp"), None),
            P("section", ("expert", "dp"), None),
            P("section", "dp", "expert"),
            P("section", "dp", "expert"),
            P("section", "expert", "dp"),
        ),
        out_specs=(
            P("section", ("expert", "dp"), None),
            P("section", "dp", "expert"),
            P("section", "dp", "expert"),
            P("section", "expert", "dp"),
        ),
        check_vma=False,
    )
```

```python
import functools

import jax
import jax.numpy as jnp
from jax import lax
from jax.experimental import pallas as pl
from jax.experimental.pallas import tpu as pltpu
from jax.sharding import PartitionSpec as P

EXPERTS = 4
CAP = 48
SHARES = 4
RING = 8
LAG = 3
X_LAST = LAG + 8
STEPS = X_LAST + 2
COLS = 256
MESH = pl.DeviceIdType.MESH
F32 = jnp.float32
BF16 = jnp.bfloat16


def dot(a, b, dim_a, dim_b):
    return lax.dot_general(a, b, (((dim_a,), (dim_b,)), ((), ())), preferred_element_type=F32)


def slots_of(chosen):
    n_tok = chosen.shape[1]
    experts = lax.broadcasted_iota(jnp.int32, (8, n_tok), 0)
    choose = jnp.where(experts == chosen, 1.0, 0.0)
    earlier = lax.broadcasted_iota(jnp.int32, (n_tok, n_tok), 0) < lax.broadcasted_iota(
        jnp.int32, (n_tok, n_tok), 1
    )
    before = dot(choose.astype(BF16), jnp.where(earlier, 1.0, 0.0).astype(BF16), 1, 0)
    slot = jnp.sum(choose * before, axis=0, keepdims=True).astype(jnp.int32)
    return jnp.broadcast_to(chosen * CAP + slot, (8, n_tok))


def places(row, slots=EXPERTS * CAP):
    ids = lax.broadcasted_iota(jnp.int32, (slots, row.shape[1]), 0)
    return jnp.where(ids == row, 1.0, 0.0).astype(BF16)


def kernel(
    rows_in, rows_out, weight, chosen, wg, wu, wd,
    f_out, gg_out, gu_out, gd_out,
    px, pz, pn, raw, target, far_target, near_target, xb, zb, wgu, wdn, pb, rb, d2, hd, g1, g2,
    tsem, raw_send, raw_recv, rx, ent_send, fwd_send, rr, rsend, fr, wrecv, wsend, wloc, grecv, gsend, gloc,
):
    sec, k, rep = lax.axis_index("section"), lax.axis_index("expert"), lax.axis_index("dp")
    mirror = lax.axis_size("section") - 1 - sec
    yh, z = k // RING, k % RING
    seg, c = z // SHARES, z % SHARES
    mine = 2 * yh + seg
    other = 1 - rep
    width = xb.shape[-1]
    half = width // 2
    units = hd.shape[-1]

    def zof(pos):
        return (SHARES * seg + pos + RING) % RING

    def here(expert):
        return (sec, expert, rep)

    twin = (sec, k, other)

    def remote(src, dst, send, recv, dev):
        return pltpu.make_async_remote_copy(
            src_ref=src, dst_ref=dst, send_sem=send, recv_sem=recv, device_id=dev, device_id_type=MESH
        )

    pair = z + 1 - 2 * (z % 2)
    z_far = (1 - seg) * SHARES + jnp.where(c < 2, SHARES - 1, 0)
    at_end = (c == 0) | (c == SHARES - 1)
    inner = (c > 0) & (c < SHARES - 1)

    def entry(e, t, proxy):
        ye, te = e // 2, e % 2
        z_in = jnp.where(seg == te, z, z_far)
        src = pn.at[t] if proxy else (px, pz)[t]
        to = sec if proxy or t == 1 else mirror
        slot = pair if proxy else z
        return remote(
            src.at[e], (xb, zb)[t].at[slot, yh], ent_send.at[proxy, t, e], rx.at[t, slot, yh],
            (to, ye * RING + z_in, rep),
        )

    def entries(t, proxy, act):
        for away in (False, True):
            for e in range(EXPERTS):
                go = (seg != e % 2) & at_end if away else seg == e % 2

                @pl.when(go if t == 0 and not proxy else go & (mine != e))
                def _():
                    act(entry(e, t, proxy))

    def own_copy(e, t, proxy):
        slot = pair if proxy else z
        src = pn.at[t] if proxy else pz
        return pltpu.make_async_copy(src.at[e], (xb, zb)[t].at[slot, yh], rx.at[t, slot, yh])

    def keep(t, proxy):
        for e in range(EXPERTS):
            @pl.when(mine == e)
            def _():
                own_copy(e, t, proxy).start()

    bar = pltpu.get_barrier_semaphore()

    def greet(*dev):
        pl.semaphore_signal(bar, inc=1, device_id=dev, device_id_type=MESH)

    step_far = jnp.where(c == 0, RING - 1, 1)
    greet(*twin)
    greet(sec, (1 - yh) * RING + z, rep)
    greet(mirror, yh * RING + pair, rep)
    for ye in range(2):
        greet(sec, ye * RING + z_far, rep)
        greet(mirror, ye * RING + z, rep)

        @pl.when(at_end)
        def _():
            greet(sec, ye * RING + (z + 2 * step_far) % RING, rep)
            greet(mirror, ye * RING + z_far, rep)

    @pl.when(c > 0)
    def _():
        greet(*here(k - 1))

    @pl.when(c < SHARES - 1)
    def _():
        greet(*here(k + 1))

    def pack(out, placing, src, scale):
        factor = None
        if scale is not None:
            factor = jnp.sum(placing.astype(F32) * scale, axis=1, keepdims=True)
        chunk = 1024

        def one(n, _):
            cols = pl.ds(pl.multiple_of(n * chunk, chunk), chunk)
            got = dot(placing, src[:, cols], 1, 0)
            if factor is not None:
                got = factor * got
            got = got.astype(BF16)
            out[..., cols] = got.reshape(out.shape[:-1] + (chunk,))

        lax.fori_loop(0, width // chunk, one, None)

    target[...] = slots_of(chosen[...])
    n_tok = raw.shape[1]

    @pl.when(inner)
    def _():
        tokens = lax.broadcasted_iota(jnp.int32, (1, n_tok), 1)
        pack(raw.at[1], places(tokens, n_tok), rows_out, weight[...])

    pack(pz, places(target[0:1, :]), rows_out, weight[...])
    pl.semaphore_wait(bar, jnp.where(at_end, 12, 9))

    near = here(yh * RING + pair)
    raw_copies = (
        remote(target, near_target, raw_send.at[0], raw_recv.at[0], near),
        remote(raw.at[1], raw.at[1], raw_send.at[1], raw_recv.at[1], near),
        remote(rows_in, raw.at[0], raw_send.at[2], raw_recv.at[2], (mirror, yh * RING + pair, rep)),
    )
    keep(1, 0)
    send_target = remote(target, far_target, tsem.at[0], tsem.at[1], (mirror, k, rep))
    send_target.start()

    @pl.when(inner)
    def _():
        raw_copies[0].start()
        raw_copies[1].start()

    entries(1, 0, lambda copy: copy.start())

    @pl.when(inner)
    def _():
        raw_copies[2].start()

    def enter_near(t):
        if t == 1:
            raw_copies[0].wait_recv()
        raw_copies[2 - t].wait_recv()
        pack(pn.at[t], places(near_target[0:1, :]), raw.at[t], None)
        keep(t, 1)
        entries(t, 1, lambda copy: copy.start())

    rows = pl.ds(pl.multiple_of(rep * half, half), half)
    rows_far = pl.ds(pl.multiple_of(other * half, half), half)
    w_parts = (
        (wg, lambda r: wgu.at[r, pl.ds(0, units)]),
        (wu, lambda r: wgu.at[r, pl.ds(units, units)]),
        (wd, lambda r: wdn.at[:, r]),
    )
    for i, (src, dst) in enumerate(w_parts):
        pltpu.make_async_copy(src, dst(rows), wloc.at[i]).start()
        remote(src, dst(rows), wsend.at[i], wrecv.at[i], twin).start()

    send_target.wait_recv()
    pack(px, places(far_target[0:1, :]), rows_in, None)
    entries(0, 0, lambda copy: copy.start())

    right, left = here(k + 1), here(k - 1)

    def forward(t, zz, y, side):
        buf = (xb, zb)[t]
        return remote(
            buf.at[zz, y], buf.at[zz, y], fwd_send.at[t, side, zz, y], rx.at[t, zz, y], (left, right)[side]
        )

    halves = (yh, 1 - yh)
    backward = (1 - yh, yh)

    def landed(t, zz, y):
        buf = (xb, zb)[t]
        remote(buf.at[zz, y], buf.at[zz, y], fwd_send.at[t, 0, zz, y], rx.at[t, zz, y], twin).wait_recv()

    onward = (c > 0, c < SHARES - 1)
    own_onward = (c >= 2, c <= 1)

    def compute(zz):
        n_rows = 2 * CAP
        x = xb[zz].reshape(n_rows, width)
        gu = dot(x, wgu[...], 1, 0)
        back = dot(zb[zz].reshape(n_rows, width), wdn[...], 1, 1)
        gate, up = gu[:, :units], gu[:, units:]
        sig = jax.nn.sigmoid(gate)
        act = gate * sig
        hd[zz] = (act * up).astype(BF16)
        d_gate = (back * up * sig * (1.0 + gate * (1.0 - sig))).astype(BF16)
        d_up = (back * act).astype(BF16)
        d2[zz, :, :units] = d_gate
        d2[zz, :, units:] = d_up
        d = jnp.concatenate([d_gate, d_up], axis=1)
        chunk = 1024

        def part(n, _):
            cols = pl.ds(pl.multiple_of(n * chunk, chunk), chunk)
            pb[zz, :, :, cols] = dot(d, wgu[cols, :], 1, 1).astype(BF16).reshape(2, CAP, chunk)

        lax.fori_loop(0, width // chunk, part, None)

    def go_back(src, zz, y, side, at_end):
        slot = jnp.where(at_end, RING, zz) if side else zz
        return remote(
            src.at[zz, y], rb.at[slot, y], rsend.at[zz, y], rr.at[slot, y], (left, right)[side]
        )

    def go_home(src, zz, y):
        return remote(
            src.at[zz, y], f_out.at[mine], rsend.at[zz, y], fr.at[mine], here(y * RING + zz)
        )

    def add_part(zz, y):
        rb[zz, y] = (rb[zz, y].astype(F32) + pb[zz, y].astype(F32)).astype(BF16)

    def wait_back(slot, y):
        remote(rb.at[slot, y], rb.at[slot, y], rsend.at[0, 0], rr.at[slot, y], twin).wait_recv()

    last = STEPS - 1

    def z_moves(j):
        return (c - j, (j >= 1) & (j <= c + 2)), (c + j, (j >= 1) & (j <= 5 - c))

    def x_moves(j):
        p_left, p_right = j - LAG - 2 - c, X_LAST - j - c
        return (p_left, (p_left >= -2) & (p_left < c)), (p_right, (p_right <= 5) & (p_right > c))

    def back_moves(j):
        p_right, p_left = j - last + c, c + last - j
        return (p_right, (c < 3) & (p_right >= -2) & (p_right <= c)), (p_left, (c > 0) & (p_left <= 5) & (p_left >= c))

    def home_copy():
        return pltpu.make_async_copy(pb.at[z, yh], f_out.at[mine], fr.at[mine])

    def weight_cols(m):
        return pl.ds(pl.multiple_of(m * COLS, COLS), COLS)

    n_all = RING * 2 * CAP

    def grads_in(m, _):
        cols = weight_cols(m)
        xt = xb[:, :, :, cols].reshape(n_all, COLS)
        wgu[cols, :] = dot(xt, d2[...].reshape(n_all, 2 * units), 0, 0).astype(BF16)

    def grads_down(m, _):
        cols = weight_cols(m)
        zt = zb[:, :, :, cols].reshape(n_all, COLS)
        wdn[:, cols] = dot(hd[...].reshape(n_all, units), zt, 0, 0).astype(BF16)

    per_half = half // COLS
    send_in = remote(wgu.at[rows_far], g1, gsend.at[0], grecv.at[0], twin)
    send_down = remote(wdn.at[:, rows_far], g2, gsend.at[1], grecv.at[1], twin)

    def step(j, _):
        (z_l, z_in_left), (z_r, z_in_right) = z_moves(j)
        (x_l, x_in_left), (x_r, x_in_right) = x_moves(j)
        (b_r, from_right), (b_l, from_left) = back_moves(j)

        @pl.when(j == 0)
        def _():
            for y in halves:
                landed(1, z, y)
                for side in range(2):
                    @pl.when(own_onward[side])
                    def _():
                        forward(1, z, y, side).start()

        for y in halves:
            for pos, valid, side in ((z_l, z_in_left, 1), (z_r, z_in_right, 0)):
                @pl.when(valid & onward[side])
                def _():
                    landed(1, zof(pos), y)
                    forward(1, zof(pos), y, side).start()

        for t in (1, 0):
            @pl.when((j == 2 - t) & at_end)
            def _():
                enter_near(t)

        @pl.when(j == LAG)
        def _():
            for y in halves:
                landed(0, z, y)
            for i, (src, dst) in enumerate(w_parts):
                pltpu.make_async_copy(src, dst(rows), wloc.at[i]).wait()
                remote(src, dst(rows_far), wsend.at[i], wrecv.at[i], twin).wait_recv()

        for y in halves:
            for pos, valid, side in ((x_l, x_in_left, 1), (x_r, x_in_right, 0)):
                @pl.when(valid)
                def _():
                    landed(0, zof(pos), y)

                @pl.when((valid & onward[side]) | ((pos == c) & own_onward[side]))
                def _():
                    forward(0, zof(pos), y, side).start()

                @pl.when(valid & ~onward[side])
                def _():
                    landed(1, zof(pos), y)

        def side_step(side, _):
            pos = jnp.where(side == 2, c, jnp.where(side == 0, x_l, x_r))
            valid = ((side == 0) & x_in_left) | ((side == 1) & x_in_right) | ((side == 2) & (j == LAG))

            @pl.when(valid)
            def _():
                zz = zof(pos)
                compute(zz)

                @pl.when((side == 0) & (c == 3))
                def _():
                    for y in backward:
                        go_back(pb, zz, y, 0, False).start()

                @pl.when((side == 1) & (c == 0))
                def _():
                    for y in backward:
                        go_back(pb, zz, y, 1, pos == 1).start()

        lax.fori_loop(0, 3, side_step, None)

        for y in backward:
            @pl.when(from_right)
            def _():
                zz = zof(b_r)
                wait_back(zz, y)

                @pl.when(b_r < c)
                def _():
                    add_part(zz, y)

                    @pl.when(c > 0)
                    def _():
                        go_back(rb, zz, y, 0, False).start()

                    @pl.when(c == 0)
                    def _():
                        go_home(rb, zz, y).start()

            @pl.when(from_left)
            def _():
                zz = zof(b_l)

                @pl.when(b_l == c)
                def _():
                    wait_back(RING, y)

                @pl.when(b_l > c)
                def _():
                    wait_back(zz, y)
                    add_part(zz, y)

                    @pl.when(c < 3)
                    def _():
                        go_back(rb, zz, y, 1, b_l == c + 1).start()

                    @pl.when(c == 3)
                    def _():
                        go_home(rb, zz, y).start()

            @pl.when(j == last)
            def _():
                @pl.when(c == 0)
                def _():
                    pb[z, y] = (pb[z, y].astype(F32) + rb[z, y].astype(F32)).astype(BF16)

                @pl.when(c == 3)
                def _():
                    pb[z, y] = (pb[z, y].astype(F32) + rb[RING, y].astype(F32)).astype(BF16)

                @pl.when((c > 0) & (c < 3))
                def _():
                    total = pb[z, y].astype(F32) + rb[z, y].astype(F32)
                    pb[z, y] = (total + rb[RING, y].astype(F32)).astype(BF16)

                if y is yh:
                    home_copy().start()
                else:
                    go_home(pb, z, y).start()

        @pl.when(j == jnp.where(inner, X_LAST - 2, X_LAST - 1))
        def _():
            lax.fori_loop(other * per_half, (other + 1) * per_half, grads_in, None)
            send_in.start()

        @pl.when(j == jnp.where(inner, X_LAST - 2, X_LAST - 1))
        def _():
            lax.fori_loop(other * per_half, (other + 1) * per_half, grads_down, None)
            send_down.start()

        @pl.when(j == jnp.where(inner, X_LAST - 2, X_LAST - 1))
        def _():
            lax.fori_loop(rep * per_half, (rep + 1) * per_half, grads_in, None)

        @pl.when(j == jnp.where(inner, X_LAST - 2, X_LAST - 1))
        def _():
            lax.fori_loop(rep * per_half, (rep + 1) * per_half, grads_down, None)

    lax.fori_loop(0, STEPS, step, None)

    piece = 512

    send_in.wait_recv()

    def add_in(m, _):
        at = pl.ds(pl.multiple_of(m * piece, piece), piece)
        own = wgu[pl.ds(pl.multiple_of(rep * half + m * piece, piece), piece), :]
        g1[at, :] = (g1[at, :].astype(F32) + own.astype(F32)).astype(BF16)

    lax.fori_loop(0, half // piece, add_in, None)
    outs = [
        pltpu.make_async_copy(g1.at[:, pl.ds(0, units)], gg_out, gloc.at[0]),
        pltpu.make_async_copy(g1.at[:, pl.ds(units, units)], gu_out, gloc.at[1]),
        pltpu.make_async_copy(g2, gd_out, gloc.at[2]),
    ]
    outs[0].start()
    outs[1].start()
    send_down.wait_recv()

    def add_down(m, _):
        at = pl.ds(pl.multiple_of(m * piece, piece), piece)
        own = wdn[:, pl.ds(pl.multiple_of(rep * half + m * piece, piece), piece)]
        g2[:, at] = (g2[:, at].astype(F32) + own.astype(F32)).astype(BF16)

    lax.fori_loop(0, half // piece, add_down, None)
    outs[2].start()

    for t in range(2):
        entries(t, 0, lambda copy: copy.wait_send())

        @pl.when(at_end)
        def _():
            entries(t, 1, lambda copy: copy.wait_send())

    @pl.when(inner)
    def _():
        for copy in raw_copies:
            copy.wait_send()

    for i, (src, dst) in enumerate(w_parts):
        remote(src, dst(rows), wsend.at[i], wrecv.at[i], twin).wait_send()
    send_target.wait_send()
    send_in.wait_send()
    send_down.wait_send()

    def drain(j, _):
        (z_l, z_in_left), (z_r, z_in_right) = z_moves(j)
        (x_l, x_in_left), (x_r, x_in_right) = x_moves(j)
        (b_r, from_right), (b_l, from_left) = back_moves(j)

        def sent(go, copy):
            @pl.when(go)
            def _():
                copy().wait_send()

        for y in halves:
            sent((z_in_left & onward[1]) | ((j == 0) & own_onward[1]), lambda: forward(1, zof(z_l), y, 1))
            sent((z_in_right & onward[0]) | ((j == 0) & own_onward[0]), lambda: forward(1, zof(z_r), y, 0))
            sent((x_in_left & onward[1]) | ((x_l == c) & own_onward[1]), lambda: forward(0, zof(x_l), y, 1))
            sent((x_in_right & onward[0]) | ((x_r == c) & own_onward[0]), lambda: forward(0, zof(x_r), y, 0))
            sent(x_in_left & (c == 3), lambda: go_back(pb, zof(x_l), y, 0, False))
            sent(x_in_right & (c == 0), lambda: go_back(pb, zof(x_r), y, 1, False))
            sent(from_right & (b_r < c) & (c > 0), lambda: go_back(rb, zof(b_r), y, 0, False))
            sent(from_left & (b_l > c) & (c < 3), lambda: go_back(rb, zof(b_l), y, 1, False))
            sent(from_right & (b_r < c) & (c == 0), lambda: go_home(rb, zof(b_r), y))
            sent(from_left & (b_l > c) & (c == 3), lambda: go_home(rb, zof(b_l), y))

    lax.fori_loop(0, STEPS, drain, None)
    go_home(pb, z, 1 - yh).wait_send()
    for e in range(EXPERTS):
        remote(f_out.at[e], f_out.at[e], rsend.at[0, 0], fr.at[e], twin).wait_recv()
    for out in outs:
        out.wait()


def finish_kernel(merged, chosen, gg, gu, gd, gi_out, gg_out, gu_out, gd_out):
    placing = places(slots_of(chosen[...])[0:1, :])
    gi_out[...] = dot(placing, merged[...], 0, 0).astype(BF16)
    gg_out[...] = gg[...]
    gu_out[...] = gu[...]
    gd_out[...] = gd[...]


def body(saved_rows, grad_out, expert_ids, combine, w_gate, w_up, w_down):
    tokens, width = saved_rows.shape[1:]
    units = w_gate.shape[2]
    half = width // 2
    chosen = expert_ids.reshape(1, tokens)
    weight = combine.reshape(1, tokens)
    dma = pltpu.SemaphoreType.DMA
    anywhere = pl.BlockSpec(memory_space=pl.ANY)
    in_vmem = pl.BlockSpec(memory_space=pltpu.VMEM)
    grad_shapes = (
        jax.ShapeDtypeStruct((half, units), BF16),
        jax.ShapeDtypeStruct((half, units), BF16),
        jax.ShapeDtypeStruct((units, half), BF16),
    )
    merged, *grads = pl.pallas_call(
        kernel,
        out_shape=(jax.ShapeDtypeStruct((EXPERTS, CAP, width), BF16),) + grad_shapes,
        in_specs=[in_vmem] * 4 + [anywhere] * 3,
        out_specs=[anywhere] * 4,
        scratch_shapes=[
            pltpu.VMEM((EXPERTS, CAP, width), BF16),
            pltpu.VMEM((EXPERTS, CAP, width), BF16),
            pltpu.VMEM((2, EXPERTS, CAP, width), BF16),
            pltpu.VMEM((2, tokens, width), BF16),
            pltpu.VMEM((8, tokens), jnp.int32),
            pltpu.VMEM((8, tokens), jnp.int32),
            pltpu.VMEM((8, tokens), jnp.int32),
            pltpu.VMEM((RING, 2, CAP, width), BF16),
            pltpu.VMEM((RING, 2, CAP, width), BF16),
            pltpu.VMEM((width, 2 * units), BF16),
            pltpu.VMEM((units, width), BF16),
            pltpu.VMEM((RING, 2, CAP, width), BF16),
            pltpu.VMEM((RING + 1, 2, CAP, width), BF16),
            pltpu.VMEM((RING, 2 * CAP, 2 * units), BF16),
            pltpu.VMEM((RING, 2 * CAP, units), BF16),
            pltpu.VMEM((half, 2 * units), BF16),
            pltpu.VMEM((units, half), BF16),
            dma((2,)),
            dma((3,)),
            dma((3,)),
            dma((2, RING, 2)),
            dma((2, 2, EXPERTS)),
            dma((2, 2, RING, 2)),
            dma((RING + 1, 2)),
            dma((RING, 2)),
            dma((EXPERTS,)),
            dma((3,)),
            dma((3,)),
            dma((3,)),
            dma((2,)),
            dma((2,)),
            dma((3,)),
        ],
        compiler_params=pltpu.CompilerParams(
            collective_id=0, has_side_effects=True, vmem_limit_bytes=60 * 1024 * 1024
        ),
    )(saved_rows[0], grad_out[0], weight, chosen, w_gate[0], w_up[0], w_down[0])
    steps = 2
    slots = EXPERTS * CAP
    row_spec = pl.BlockSpec((half // steps, units), lambda i: (i, 0))
    grad_specs = [row_spec, row_spec, pl.BlockSpec((units // steps, half), lambda i: (i, 0))]
    grad_in, *grads = pl.pallas_call(
        finish_kernel,
        grid=(steps,),
        out_shape=(jax.ShapeDtypeStruct((tokens, width), BF16),) + grad_shapes,
        in_specs=[
            pl.BlockSpec((slots, width // steps), lambda i: (0, i)),
            pl.BlockSpec((1, tokens), lambda i: (0, 0)),
        ]
        + grad_specs,
        out_specs=[pl.BlockSpec((tokens, width // steps), lambda i: (0, i))] + grad_specs,
        compiler_params=pltpu.CompilerParams(vmem_limit_bytes=60 * 1024 * 1024),
    )(merged.reshape(slots, width), chosen, *grads)
    return grad_in[None], *(grad[None] for grad in grads)


def solution(mesh):
    return jax.shard_map(
        body,
        mesh=mesh,
        in_specs=(
            P("section", ("expert", "dp"), None),
            P("section", ("expert", "dp"), None),
            P("section", ("expert", "dp"), None),
            P("section", ("expert", "dp"), None),
            P("section", "dp", "expert"),
            P("section", "dp", "expert"),
            P("section", "expert", "dp"),
        ),
        out_specs=(
            P("section", ("expert", "dp"), None),
            P("section", "dp", "expert"),
            P("section", "dp", "expert"),
            P("section", "expert", "dp"),
        ),
        check_vma=False,
    )
```
